32 devices in a mesh: slide: 8 (over z, x), rep: 4 (over y, core).
Axes of the slice: x: 2, y: 2, z: 4, core: 2. Of those that a mesh axis runs over, the one named last changes fastest.
Arguments:
- tile_feats: bfloat16 [128, 8, 8, 192], P(('slide', 'rep'))
- cotangent: bfloat16 [128, 4, 4, 384], P(('slide', 'rep')), may hold values from -0.125 to 0.125
- keep_list: int32 [32, 4], P(('slide', 'rep')), may hold values from 0 to 3, each once within a row
- tile_plan: int32 [32, 2], P(('slide', 'rep')), may hold values from 0 to 4, as said below
- kernel_one: bfloat16 [7, 7, 192], replicated, may hold values from -0.875 to 0.875
- gain_one: bfloat16 [192], replicated, may hold values from 0.25 to 1.75
- inward_one: bfloat16 [192, 768], replicated, may hold values from -0.4375 to 0.4375
- outward_one: bfloat16 [768, 192], replicated, may hold values from -0.21875 to 0.21875
- gain_down: bfloat16 [192], replicated, may hold values from 0.25 to 1.75
- project_down: bfloat16 [768, 384], replicated, may hold values from -0.21875 to 0.21875
- kernel_two: bfloat16 [7, 7, 384], replicated, may hold values from -0.875 to 0.875
- gain_two: bfloat16 [384], replicated, may hold values from 0.25 to 1.75
- inward_two: bfloat16 [384, 1536], replicated, may hold values from -0.3125 to 0.3125
- outward_two: bfloat16 [1536, 384], replicated, may hold values from -0.15625 to 0.15625
Outputs:
- features: bfloat16 [128, 4, 4, 384], P(('slide', 'rep'))
- grad_inward: float32 [192, 768], P(None, 'slide')
- grad_outward: float32 [768, 192], P('slide')
- grad_project: float32 [768, 384], P('slide')
The draws below stay inside these ranges and needn't reach their ends.
Inputs may be any that keep to these rules, and one draw needn't show every extreme that they name: `keep_list`: each row is a permutation of 0 to 3. `tile_plan`: column 0 counts the device's kept tiles, column 1 is its partner bit, from 0 to 2. The device at the same rep index whose slide index differs only in that bit is its partner and has the same partner bit; the bit is the same over each aligned group of 8 slide indices. Partners' counts sum to at most 4. In every replica some device keeps 4 tiles and its partner none.
All inputs are finite; a program needn't handle non-finite values.
Results may differ from the reference program's by a relative error of at most 0.018.
Values may be sent and summed in bfloat16 or wider, within the bound.
A program may use at most 64 MiB of HBM per device.

```python
import jax
import jax.numpy as jnp
from jax import lax

C1 = 192
C2 = 384
KSIZE = 7
HID1 = 768
HID2 = 1536
S1 = 8
S2 = 4
CAP = 2
CAND = 4
SLIDES = 8
REPLICAS = 4
GROUPS = 32
TILES = 128


def draw_tile_feats(key, part):
    first, second, third = jax.random.split(key, 3)
    shape = (TILES, S1, S1, C1)
    base = jax.random.normal(first, shape, jnp.float32)
    channel = jnp.exp(jax.random.uniform(second, (C1,), jnp.float32, 0.0, 2.3)) * 0.3
    cell = jnp.exp(jax.random.uniform(third, (TILES, S1, S1, 1), jnp.float32, 0.0, 2.3)) * 0.3
    return (base * channel * cell).astype(jnp.bfloat16)


def draw_tile_plan(key, part):
    base = jax.random.fold_in(key, 11)
    first, second, third, fourth = jax.random.split(base, 4)
    slide_index = jnp.arange(SLIDES, dtype=jnp.int32)[:, None] + jnp.zeros((1, REPLICAS), jnp.int32)
    replica = jnp.arange(REPLICAS, dtype=jnp.int32)[None, :] + jnp.zeros((SLIDES, 1), jnp.int32)
    bit_table = jax.random.randint(first, (SLIDES // 8, REPLICAS), 0, 3)
    bit_table = bit_table.at[0, 0].set(2).at[0, 1].set(0)
    partner_bits = bit_table[slide_index // 8, replica]
    stride = jnp.left_shift(jnp.ones_like(partner_bits), partner_bits)
    upper = slide_index // stride % 2
    leader = slide_index - upper * stride
    kinds = jax.random.randint(second, (SLIDES, REPLICAS), 0, 3)[leader, replica]
    kinds = jnp.where(leader == 0, 0, kinds)
    flips = jax.random.randint(third, (SLIDES, REPLICAS), 0, 2)[leader, replica]
    spares = jax.random.randint(fourth, (SLIDES, REPLICAS), 0, CAP + 1)[leader, replica]
    heavy = jnp.where(kinds == 0, 2 * CAP, jnp.where(kinds == 1, 2 * CAP - 1, CAP))
    light = jnp.where(kinds == 0, 0, jnp.where(kinds == 1, 1, spares))
    counts = jnp.where(upper == flips, heavy, light)
    return jnp.stack([counts, partner_bits], axis=-1).reshape(SLIDES * REPLICAS, 2).astype(jnp.int32)


def levels(rng, dims, pieces, low, top_value):
    level = 1.0
    for dim, parts in pieces:
        heights = jax.random.uniform(jax.random.fold_in(jax.random.fold_in(rng, 6), dim), (parts,), jnp.float32, low / len(pieces), top_value / len(pieces))
        level = level * jnp.repeat(jnp.exp(heights), dims[dim] // parts).reshape((-1,) + (1,) * (len(dims) - 1 - dim))
    return level


def centred(key, extent, width, reach, cuts=(), kind=jnp.bfloat16):
    drawn = width * jax.random.normal(key, extent, jnp.float32)
    if cuts:
        drawn = drawn * levels(key, extent, cuts, -0.22, 0.18)
    return jnp.clip(drawn, -reach, reach).astype(kind)


def setup_inputs(seed: int = 0) -> dict:
    seeds = jax.random.split(jax.random.key(seed), 15)
    return {
        "tile_feats": draw_tile_feats(jax.random.fold_in(seeds[14], 71), 0),
        "cotangent": centred(seeds[1], (TILES, S2, S2, C2), (2.0 * (S1 * S1 * CAND * GROUPS) ** -0.5), 0.125, ((0, 32),)),
        "keep_list": jax.vmap(lambda own: jax.random.permutation(own, CAND))(jax.random.split(seeds[2], GROUPS)).reshape((GROUPS, CAND)).astype(jnp.int32),
        "tile_plan": draw_tile_plan(jax.random.fold_in(seeds[14], 71), 0),
        "kernel_one": centred(seeds[4], (KSIZE, KSIZE, C1), (KSIZE * KSIZE) ** -0.5, 0.875),
        "gain_one": jnp.clip(1.0 + 0.15 * jax.random.normal(seeds[5], (C1,), jnp.float32), 0.25, 1.75).astype(jnp.bfloat16),
        "inward_one": centred(seeds[6], (C1, HID1), C1 ** -0.5, 0.4375),
        "outward_one": centred(seeds[7], (HID1, C1), HID1 ** -0.5, 0.21875),
        "gain_down": jnp.clip(1.0 + 0.15 * jax.random.normal(seeds[8], (C1,), jnp.float32), 0.25, 1.75).astype(jnp.bfloat16),
        "project_down": centred(seeds[9], (4 * C1, C2), (4 * C1) ** -0.5, 0.21875),
        "kernel_two": centred(seeds[10], (KSIZE, KSIZE, C2), (KSIZE * KSIZE) ** -0.5, 0.875),
        "gain_two": jnp.clip(1.0 + 0.15 * jax.random.normal(seeds[11], (C2,), jnp.float32), 0.25, 1.75).astype(jnp.bfloat16),
        "inward_two": centred(seeds[12], (C2, HID2), C2 ** -0.5, 0.3125),
        "outward_two": centred(seeds[13], (HID2, C2), HID2 ** -0.5, 0.15625),
    }


def depthwise(field, kernel):
    return lax.conv_general_dilated(field.astype(jnp.float32), kernel.astype(jnp.float32)[:, :, None, :], (1, 1), 'SAME', dimension_numbers=('NHWC', 'HWIO', 'NHWC'), feature_group_count=field.shape[-1], precision=lax.Precision.HIGHEST)

def layer_norm(values, gain):
    centre = lax.optimization_barrier(jnp.mean(values, axis=-1, keepdims=True))
    offset = values - centre
    spread = lax.optimization_barrier(jnp.mean(offset * offset, axis=-1, keepdims=True))
    return offset * lax.rsqrt(spread + 1e-06) * gain.astype(jnp.float32)

def gelu_exact(values):
    return jax.nn.gelu(values, approximate=False)

def slot_pass(tile_feats, cotangent, weights):
    kernel_one, gain_one, inward_one, outward_one, gain_down, project_down, kernel_two, gain_two, inward_two, outward_two = weights
    slot_count = tile_feats.shape[0]
    side_cells = tile_feats.shape[1]
    narrow_width = tile_feats.shape[3]
    half_side = side_cells // 2
    wide_width = project_down.shape[1]
    first_rows = slot_count * side_cells * side_cells
    second_rows = slot_count * half_side * half_side
    normed = layer_norm(depthwise(tile_feats, kernel_one), gain_one).astype(jnp.bfloat16).reshape(first_rows, narrow_width)
    expand = jnp.dot(normed, inward_one, preferred_element_type=jnp.float32)
    hidden = gelu_exact(expand).astype(jnp.bfloat16)
    flat_input = tile_feats.reshape(first_rows, narrow_width)
    section_one = (flat_input.astype(jnp.float32) + jnp.dot(hidden, outward_one, preferred_element_type=jnp.float32)).astype(jnp.bfloat16)
    down_normed = layer_norm(section_one.astype(jnp.float32), gain_down).astype(jnp.bfloat16)
    patches = down_normed.reshape(slot_count, half_side, 2, half_side, 2, narrow_width).transpose(0, 1, 3, 2, 4, 5).reshape(second_rows, 4 * narrow_width)
    merged = jnp.dot(patches, project_down, preferred_element_type=jnp.float32).astype(jnp.bfloat16)
    merged_grid = merged.reshape(slot_count, half_side, half_side, wide_width).astype(jnp.float32)

    def second_norm(values):
        return layer_norm(depthwise(values, kernel_two), gain_two)
    normed_two = second_norm(merged_grid).astype(jnp.bfloat16).reshape(second_rows, wide_width)
    expand_two = jnp.dot(normed_two, inward_two, preferred_element_type=jnp.float32)
    hidden_two = gelu_exact(expand_two).astype(jnp.bfloat16)
    features = (merged.astype(jnp.float32) + jnp.dot(hidden_two, outward_two, preferred_element_type=jnp.float32)).astype(jnp.bfloat16)
    flat_cot = cotangent.reshape(second_rows, wide_width)
    back_hidden_two = jnp.dot(flat_cot, outward_two.T, preferred_element_type=jnp.float32).astype(jnp.bfloat16)
    unused, gelu_back_two = jax.vjp(gelu_exact, expand_two)
    back_expand_two = gelu_back_two(back_hidden_two.astype(jnp.float32))[0].astype(jnp.bfloat16)
    back_normed_two = jnp.dot(back_expand_two, inward_two.T, preferred_element_type=jnp.float32).astype(jnp.bfloat16)
    unused, norm_back_two = jax.vjp(second_norm, merged_grid)
    back_depth = norm_back_two(back_normed_two.astype(jnp.float32).reshape(slot_count, half_side, half_side, wide_width))[0]
    back_merged = (flat_cot.astype(jnp.float32) + back_depth.reshape(second_rows, wide_width)).astype(jnp.bfloat16)
    grad_project = jnp.dot(patches.T, back_merged, preferred_element_type=jnp.float32)
    back_patches = jnp.dot(back_merged, project_down.T, preferred_element_type=jnp.float32).astype(jnp.bfloat16)
    back_down = back_patches.reshape(slot_count, half_side, half_side, 2, 2, narrow_width).transpose(0, 1, 3, 2, 4, 5).reshape(first_rows, narrow_width)
    unused, norm_back_down = jax.vjp(lambda values: layer_norm(values, gain_down), section_one.astype(jnp.float32))
    back_section = norm_back_down(back_down.astype(jnp.float32))[0].astype(jnp.bfloat16)
    grad_outward = jnp.dot(hidden.T, back_section, preferred_element_type=jnp.float32)
    back_hidden = jnp.dot(back_section, outward_one.T, preferred_element_type=jnp.float32).astype(jnp.bfloat16)
    unused, gelu_back = jax.vjp(gelu_exact, expand)
    back_expand = gelu_back(back_hidden.astype(jnp.float32))[0].astype(jnp.bfloat16)
    grad_inward = jnp.dot(normed.T, back_expand, preferred_element_type=jnp.float32)
    return (features.reshape(slot_count, half_side, half_side, wide_width), grad_inward, grad_outward, grad_project)

def column_mask(mask, rank):
    return mask.reshape(mask.shape + (1,) * rank)

def fill_slots(own_rows, partner_rows, own_number, partner_number):
    capacity = own_rows.shape[0]
    slot_index = jnp.arange(capacity, dtype=jnp.int32)
    take_own = slot_index < own_number
    shifted = jnp.clip(slot_index - own_number, 0, capacity - 1)
    take_partner = jnp.logical_and(slot_index >= own_number, slot_index - own_number < partner_number)
    rank = own_rows.ndim - 1
    zero_value = jnp.zeros((), own_rows.dtype)
    return jnp.where(column_mask(take_own, rank), own_rows, jnp.where(column_mask(take_partner, rank), partner_rows[shifted], zero_value))

def reference(tile_feats, cotangent, keep_list, tile_plan, kernel_one, gain_one, inward_one, outward_one, gain_down, project_down, kernel_two, gain_two, inward_two, outward_two):
    weights = (kernel_one, gain_one, inward_one, outward_one, gain_down, project_down, kernel_two, gain_two, inward_two, outward_two)
    group_total = keep_list.shape[0]
    candidates = keep_list.shape[1]
    capacity = candidates // 2
    side_cells = tile_feats.shape[1]
    narrow_width = tile_feats.shape[3]
    half_side = cotangent.shape[1]
    wide_width = cotangent.shape[3]
    tile_blocks = tile_feats.reshape(group_total, candidates, side_cells, side_cells, narrow_width)
    cot_blocks = cotangent.reshape(group_total, candidates, half_side, half_side, wide_width)
    counts = tile_plan[:, 0]
    partner_bits = tile_plan[:, 1]
    positions = jnp.arange(candidates, dtype=jnp.int32)
    live = positions[None, :] < counts[:, None]
    zero_value = jnp.zeros((), jnp.bfloat16)
    ordered_tiles = jnp.where(column_mask(live, 3), jax.vmap(lambda block_rows, ordering: block_rows[ordering])(tile_blocks, keep_list), zero_value)
    ordered_cot = jnp.where(column_mask(live, 3), jax.vmap(lambda block_rows, ordering: block_rows[ordering])(cot_blocks, keep_list), zero_value)
    group_index = jnp.arange(group_total, dtype=jnp.int32)
    slide_index = group_index // REPLICAS
    replica = group_index % REPLICAS
    partner = jnp.bitwise_xor(slide_index, jnp.left_shift(jnp.ones_like(partner_bits), partner_bits)) * REPLICAS + replica
    own_numbers = jnp.minimum(counts, capacity)
    extra_numbers = jnp.clip(counts - capacity, 0, capacity)

    def step(totals, group):
        partner_group = partner[group]
        slot_tiles = fill_slots(ordered_tiles[group, :capacity], ordered_tiles[partner_group, capacity:], own_numbers[group], extra_numbers[partner_group])
        slot_cot = fill_slots(ordered_cot[group, :capacity], ordered_cot[partner_group, capacity:], own_numbers[group], extra_numbers[partner_group])
        outcome = slot_pass(slot_tiles, slot_cot, weights)
        return ((totals[0] + outcome[1], totals[1] + outcome[2], totals[2] + outcome[3]), outcome[0])
    start = (jnp.zeros(inward_one.shape, jnp.float32), jnp.zeros(outward_one.shape, jnp.float32), jnp.zeros(project_down.shape, jnp.float32))
    totals, slot_feats = lax.scan(step, start, group_index)
    returned_index = jnp.clip(own_numbers[partner][:, None] + positions[None, :capacity], 0, capacity - 1)
    returned = slot_feats[partner[:, None], returned_index]
    position_feats = jnp.concatenate([slot_feats, returned], axis=1)
    place = lax.optimization_barrier(jnp.sum(jnp.where(keep_list[:, None, :] == positions[None, :, None], positions[None, None, :], 0), axis=2)).astype(jnp.int32)
    chosen = jax.vmap(lambda block_rows, where_at: block_rows[where_at])(position_feats, place)
    features = jnp.where(column_mask(place < counts[:, None], 3), chosen, zero_value).reshape(cotangent.shape)
    return (features, totals[0], totals[1], totals[2])
```

```python
import functools

import jax
import jax.numpy as jnp
from jax import lax
from jax.experimental import pallas as pl
from jax.experimental.pallas import tpu as pltpu
from jax.sharding import PartitionSpec as P


def depthwise(field, kernel):
    return lax.conv_general_dilated(
        field.astype(jnp.float32),
        kernel.astype(jnp.float32)[:, :, None, :],
        (1, 1),
        "SAME",
        dimension_numbers=("NHWC", "HWIO", "NHWC"),
        feature_group_count=field.shape[-1],
        precision=lax.Precision.HIGHEST,
    )


def layer_norm(values, gain):
    centre = jnp.mean(values, axis=-1, keepdims=True)
    offset = values - centre
    spread = jnp.mean(offset * offset, axis=-1, keepdims=True)
    return offset * lax.rsqrt(spread + 1e-06) * gain.astype(jnp.float32)


def gelu_exact(values):
    return jax.nn.gelu(values, approximate=False)


def slot_pass(tile_feats, cotangent, weights):
    (
        kernel_one,
        gain_one,
        inward_one,
        outward_one,
        gain_down,
        project_down,
        kernel_two,
        gain_two,
        inward_two,
        outward_two,
    ) = weights
    slot_count = tile_feats.shape[0]
    side_cells = tile_feats.shape[1]
    narrow_width = tile_feats.shape[3]
    half_side = side_cells // 2
    wide_width = project_down.shape[1]
    first_rows = slot_count * side_cells * side_cells
    second_rows = slot_count * half_side * half_side
    normed = (
        layer_norm(depthwise(tile_feats, kernel_one), gain_one)
        .astype(jnp.bfloat16)
        .reshape(first_rows, narrow_width)
    )
    expand = jnp.dot(normed, inward_one, preferred_element_type=jnp.float32)
    hidden = gelu_exact(expand).astype(jnp.bfloat16)
    flat_input = tile_feats.reshape(first_rows, narrow_width)
    section_one = (
        flat_input.astype(jnp.float32)
        + jnp.dot(hidden, outward_one, preferred_element_type=jnp.float32)
    ).astype(jnp.bfloat16)
    down_normed = layer_norm(section_one.astype(jnp.float32), gain_down).astype(jnp.bfloat16)
    patches = (
        down_normed.reshape(slot_count, half_side, 2, half_side, 2, narrow_width)
        .transpose(0, 1, 3, 2, 4, 5)
        .reshape(second_rows, 4 * narrow_width)
    )
    merged = jnp.dot(patches, project_down, preferred_element_type=jnp.float32).astype(jnp.bfloat16)
    merged_grid = merged.reshape(slot_count, half_side, half_side, wide_width).astype(jnp.float32)

    def second_norm(values):
        return layer_norm(depthwise(values, kernel_two), gain_two)

    normed_two = second_norm(merged_grid).astype(jnp.bfloat16).reshape(second_rows, wide_width)
    expand_two = jnp.dot(normed_two, inward_two, preferred_element_type=jnp.float32)
    hidden_two = gelu_exact(expand_two).astype(jnp.bfloat16)
    features = (
        merged.astype(jnp.float32)
        + jnp.dot(hidden_two, outward_two, preferred_element_type=jnp.float32)
    ).astype(jnp.bfloat16)
    flat_cot = cotangent.reshape(second_rows, wide_width)
    back_hidden_two = jnp.dot(flat_cot, outward_two.T, preferred_element_type=jnp.float32).astype(
        jnp.bfloat16
    )
    unused, gelu_back_two = jax.vjp(gelu_exact, expand_two)
    back_expand_two = gelu_back_two(back_hidden_two.astype(jnp.float32))[0].astype(jnp.bfloat16)
    back_normed_two = jnp.dot(
        back_expand_two, inward_two.T, preferred_element_type=jnp.float32
    ).astype(jnp.bfloat16)
    unused, norm_back_two = jax.vjp(second_norm, merged_grid)
    back_depth = norm_back_two(
        back_normed_two.astype(jnp.float32).reshape(slot_count, half_side, half_side, wide_width)
    )[0]
    back_merged = (
        flat_cot.astype(jnp.float32) + back_depth.reshape(second_rows, wide_width)
    ).astype(jnp.bfloat16)
    grad_project = jnp.dot(patches.T, back_merged, preferred_element_type=jnp.float32)
    back_patches = jnp.dot(back_merged, project_down.T, preferred_element_type=jnp.float32).astype(
        jnp.bfloat16
    )
    back_down = (
        back_patches.reshape(slot_count, half_side, half_side, 2, 2, narrow_width)
        .transpose(0, 1, 3, 2, 4, 5)
        .reshape(first_rows, narrow_width)
    )
    unused, norm_back_down = jax.vjp(
        lambda values: layer_norm(values, gain_down), section_one.astype(jnp.float32)
    )
    back_section = norm_back_down(back_down.astype(jnp.float32))[0].astype(jnp.bfloat16)
    grad_outward = jnp.dot(hidden.T, back_section, preferred_element_type=jnp.float32)
    back_hidden = jnp.dot(back_section, outward_one.T, preferred_element_type=jnp.float32).astype(
        jnp.bfloat16
    )
    unused, gelu_back = jax.vjp(gelu_exact, expand)
    back_expand = gelu_back(back_hidden.astype(jnp.float32))[0].astype(jnp.bfloat16)
    grad_inward = jnp.dot(back_expand.T, normed, preferred_element_type=jnp.float32)
    return (
        features.reshape(slot_count, half_side, half_side, wide_width),
        grad_inward,
        grad_outward,
        grad_project,
    )


MESH = pl.DeviceIdType.MESH


def exchange_kernel(line, halves, out, get_pair, put_quad, get_quad, mine, put_line, get_line, put_rep, get_rep, pair_sems, quad_sems, line_sems, rep_sems):
    s = lax.axis_index("slide")
    r = lax.axis_index("rep")
    core, y = r % 2, r // 2
    x, z = s % 2, s // 2
    spot = x * 2 + y
    pair_peer = (s, y * 2 + 1 - core)

    def quad_peer(d):
        return (z * 2 + (x + d // 2) % 2, ((y + d) % 2) * 2 + core)

    def line_peer(d):
        return (((z + d) % line) * 2 + x, r)

    def rep_peer(d):
        return (s, ((y + d // 2) % 2) * 2 + (core + d) % 2)

    def quad_spot(d):
        return ((x + d // 2) % 2) * 2 + (y + d) % 2

    barrier = pltpu.get_barrier_semaphore()
    peers = [rep_peer(d) for d in (1, 2, 3)] + [quad_peer(d) for d in (2, 3)] + [line_peer(d) for d in range(1, line)]
    for peer in peers:
        pl.semaphore_signal(barrier, inc=1, device_id=peer, device_id_type=MESH)
    pl.semaphore_wait(barrier, len(peers))

    def send(src, dst, sems, slot, peer):
        copy = pltpu.make_async_remote_copy(
            src_ref=src, dst_ref=dst, send_sem=sems.at[0, slot], recv_sem=sems.at[1, slot],
            device_id=peer, device_id_type=MESH)
        copy.start()
        return copy

    pairs = {}
    for d in (3, 2, 1, 0):
        pairs[d] = send(halves.at[1 - core, quad_spot(d)], get_pair.at[d], pair_sems, d, pair_peer)
    quads = {}
    for d in (3, 2, 1):
        pairs[d].wait_recv()
        put_quad[d - 1] = (halves[core, quad_spot(d)].astype(jnp.float32) + get_pair[d].astype(jnp.float32)).astype(jnp.bfloat16)
        quads[d] = send(put_quad.at[d - 1], get_quad.at[d - 1], quad_sems, d - 1, quad_peer(d))
    pairs[0].wait_recv()
    mine[...] = halves[core, spot].astype(jnp.float32) + get_pair[0].astype(jnp.float32)
    for d in (1, 2, 3):
        quads[d].wait_recv()
    lines = {}
    for d in [*range(line - 1, 0, -1), 0]:
        at = (z + d) % line
        part = mine[at] + get_quad[0, at].astype(jnp.float32) + get_quad[1, at].astype(jnp.float32) + get_quad[2, at].astype(jnp.float32)
        if d:
            put_line[d - 1] = part.astype(jnp.bfloat16)
            lines[d] = send(put_line.at[d - 1], get_line.at[d - 1], line_sems, d - 1, line_peer(d))
        else:
            total = part
    for d in range(1, line):
        lines[d].wait_recv()
        total = total + get_line[d - 1].astype(jnp.float32)
    put_rep[...] = total.astype(jnp.bfloat16)
    reps = {}
    for d in (3, 2, 1):
        reps[d] = send(put_rep, get_rep.at[d - 1], rep_sems, d - 1, rep_peer(d))
    out[core, y] = put_rep[...].astype(jnp.float32)
    for d in (1, 3, 2):
        reps[d].wait_recv()
        out[(core + d) % 2, (y + d // 2) % 2] = get_rep[d - 1].astype(jnp.float32)
    for copy in [*pairs.values(), *quads.values(), *lines.values(), *reps.values()]:
        copy.wait_send()


def exchange(halves, slides):
    line = slides // 2
    block = halves.shape[-2:]
    return pl.pallas_call(
        functools.partial(exchange_kernel, line),
        out_shape=jax.ShapeDtypeStruct((2, 2) + block, jnp.float32),
        in_specs=[pl.BlockSpec(memory_space=pltpu.VMEM)],
        out_specs=pl.BlockSpec(memory_space=pltpu.VMEM),
        scratch_shapes=[
            pltpu.VMEM((4, line) + block, jnp.bfloat16),
            pltpu.VMEM((3, line) + block, jnp.bfloat16),
            pltpu.VMEM((3, line) + block, jnp.bfloat16),
            pltpu.VMEM((line,) + block, jnp.float32),
            pltpu.VMEM((line - 1,) + block, jnp.bfloat16),
            pltpu.VMEM((line - 1,) + block, jnp.bfloat16),
            pltpu.VMEM(block, jnp.bfloat16),
            pltpu.VMEM((3,) + block, jnp.bfloat16),
            pltpu.SemaphoreType.DMA((2, 4)),
            pltpu.SemaphoreType.DMA((2, 3)),
            pltpu.SemaphoreType.DMA((2, line - 1)),
            pltpu.SemaphoreType.DMA((2, 3)),
        ],
        compiler_params=pltpu.CompilerParams(collective_id=0, has_side_effects=True, vmem_limit_bytes=48 * 1024 * 1024),
        cost_estimate=pl.CostEstimate(flops=10**6, bytes_accessed=4 * 10**6, transcendentals=0),
    )(halves)


def shares(grad_inward_t, grad_outward, grad_project):
    slides, reps = lax.axis_size("slide"), lax.axis_size("rep")
    rows, narrow = grad_outward.shape
    both = jnp.concatenate([grad_inward_t, grad_outward], axis=1)
    if reps == 4 and slides % 2 == 0 and slides > 2 and rows % (slides * 32) == 0 and both.shape == grad_project.shape:
        line, part = slides // 2, rows // slides // 2
        halves = jnp.stack([grad_project, both]).astype(jnp.bfloat16)
        halves = halves.reshape(2, line, 4, part, -1).transpose(0, 2, 1, 3, 4)
        got = exchange(halves, slides).reshape(2, 2 * part, -1)
        project, both = got[0], got[1]
    else:
        project, both = (
            lax.psum(lax.psum_scatter(g, "slide", scatter_dimension=0, tiled=True), "rep") for g in (grad_project, both))
    return both[:, :narrow].T, both[:, narrow:], project


def column_mask(mask, rank):
    return mask.reshape(mask.shape + (1,) * rank)


def per_device(
    tile_feats,
    cotangent,
    keep_list,
    tile_plan,
    kernel_one,
    gain_one,
    inward_one,
    outward_one,
    gain_down,
    project_down,
    kernel_two,
    gain_two,
    inward_two,
    outward_two,
):
    weights = (
        kernel_one,
        gain_one,
        inward_one,
        outward_one,
        gain_down,
        project_down,
        kernel_two,
        gain_two,
        inward_two,
        outward_two,
    )
    candidates = tile_feats.shape[0]
    ordering = keep_list[0]
    kept_count = tile_plan[0, 0]
    positions = jnp.arange(candidates, dtype=jnp.int32)
    live = positions < kept_count
    zero_value = jnp.zeros((), jnp.bfloat16)
    ordered_tiles = jnp.where(column_mask(live, 3), tile_feats[ordering], zero_value)
    ordered_cot = jnp.where(column_mask(live, 3), cotangent[ordering], zero_value)
    position_feats, grad_inward, grad_outward, grad_project = slot_pass(
        ordered_tiles, ordered_cot, weights
    )
    place = jnp.sum(
        jnp.where(ordering[None, :] == positions[:, None], positions[None, :], 0), axis=1
    )
    features = jnp.where(column_mask(place < kept_count, 3), position_feats[place], zero_value)
    inward_share, outward_share, project_share = shares(grad_inward, grad_outward, grad_project)
    return (features, inward_share, outward_share, project_share)


def solution(mesh):
    in_specs = (
        P(("slide", "rep"), None, None, None),
        P(("slide", "rep"), None, None, None),
        P(("slide", "rep"), None),
        P(("slide", "rep"), None),
        P(),
        P(),
        P(),
        P(),
        P(),
        P(),
        P(),
        P(),
        P(),
        P(),
    )
    out_specs = (
        P(("slide", "rep"), None, None, None),
        P(None, "slide"),
        P("slide", None),
        P("slide", None),
    )
    return jax.shard_map(
        per_device, mesh=mesh, in_specs=in_specs, out_specs=out_specs, check_vma=False
    )
```

```python
import functools

import jax
import jax.numpy as jnp
from jax import lax
from jax.experimental import pallas as pl
from jax.experimental.pallas import tpu as pltpu
from jax.sharding import PartitionSpec as P

MESH = pl.DeviceIdType.MESH


def exchange_kernel(line, halves, out, get_pair, put_quad, get_quad, mine, put_line, get_line, put_rep, get_rep, pair_sems, quad_sems, line_sems, rep_sems):
    s = lax.axis_index("slide")
    r = lax.axis_index("rep")
    core, y = r % 2, r // 2
    x, z = s % 2, s // 2
    spot = x * 2 + y
    pair_peer = (s, y * 2 + 1 - core)

    def quad_peer(d):
        return (z * 2 + (x + d // 2) % 2, ((y + d) % 2) * 2 + core)

    def line_peer(d):
        return (((z + d) % line) * 2 + x, r)

    def rep_peer(d):
        return (s, ((y + d // 2) % 2) * 2 + (core + d) % 2)

    def quad_spot(d):
        return ((x + d // 2) % 2) * 2 + (y + d) % 2

    barrier = pltpu.get_barrier_semaphore()
    peers = [rep_peer(d) for d in (1, 2, 3)] + [quad_peer(d) for d in (2, 3)] + [line_peer(d) for d in range(1, line)]
    for peer in peers:
        pl.semaphore_signal(barrier, inc=1, device_id=peer, device_id_type=MESH)
    pl.semaphore_wait(barrier, len(peers))

    def send(src, dst, sems, slot, peer):
        copy = pltpu.make_async_remote_copy(
            src_ref=src, dst_ref=dst, send_sem=sems.at[0, slot], recv_sem=sems.at[1, slot],
            device_id=peer, device_id_type=MESH)
        copy.start()
        return copy

    pairs = {}
    for d in (3, 2, 1, 0):
        pairs[d] = send(halves.at[1 - core, quad_spot(d)], get_pair.at[d], pair_sems, d, pair_peer)
    quads = {}
    for d in (3, 2, 1):
        pairs[d].wait_recv()
        put_quad[d - 1] = (halves[core, quad_spot(d)].astype(jnp.float32) + get_pair[d].astype(jnp.float32)).astype(jnp.bfloat16)
        quads[d] = send(put_quad.at[d - 1], get_quad.at[d - 1], quad_sems, d - 1, quad_peer(d))
    pairs[0].wait_recv()
    mine[...] = halves[core, spot].astype(jnp.float32) + get_pair[0].astype(jnp.float32)
    for d in (1, 2, 3):
        quads[d].wait_recv()
    lines = {}
    for d in [*range(line - 1, 0, -1), 0]:
        at = (z + d) % line
        part = mine[at] + get_quad[0, at].astype(jnp.float32) + get_quad[1, at].astype(jnp.float32) + get_quad[2, at].astype(jnp.float32)
        if d:
            put_line[d - 1] = part.astype(jnp.bfloat16)
            lines[d] = send(put_line.at[d - 1], get_line.at[d - 1], line_sems, d - 1, line_peer(d))
        else:
            total = part
    for d in range(1, line):
        lines[d].wait_recv()
        total = total + get_line[d - 1].astype(jnp.float32)
    put_rep[...] = total.astype(jnp.bfloat16)
    reps = {}
    for d in (3, 2, 1):
        reps[d] = send(put_rep, get_rep.at[d - 1], rep_sems, d - 1, rep_peer(d))
    out[core, y] = put_rep[...].astype(jnp.float32)
    for d in (1, 3, 2):
        reps[d].wait_recv()
        out[(core + d) % 2, (y + d // 2) % 2] = get_rep[d - 1].astype(jnp.float32)
    for copy in [*pairs.values(), *quads.values(), *lines.values(), *reps.values()]:
        copy.wait_send()


def exchange(halves, slides):
    line = slides // 2
    block = halves.shape[-2:]
    return pl.pallas_call(
        functools.partial(exchange_kernel, line),
        out_shape=jax.ShapeDtypeStruct((2, 2) + block, jnp.float32),
        in_specs=[pl.BlockSpec(memory_space=pltpu.VMEM)],
        out_specs=pl.BlockSpec(memory_space=pltpu.VMEM),
        scratch_shapes=[
            pltpu.VMEM((4, line) + block, jnp.bfloat16),
            pltpu.VMEM((3, line) + block, jnp.bfloat16),
            pltpu.VMEM((3, line) + block, jnp.bfloat16),
            pltpu.VMEM((line,) + block, jnp.float32),
            pltpu.VMEM((line - 1,) + block, jnp.bfloat16),
            pltpu.VMEM((line - 1,) + block, jnp.bfloat16),
            pltpu.VMEM(block, jnp.bfloat16),
            pltpu.VMEM((3,) + block, jnp.bfloat16),
            pltpu.SemaphoreType.DMA((2, 4)),
            pltpu.SemaphoreType.DMA((2, 3)),
            pltpu.SemaphoreType.DMA((2, line - 1)),
            pltpu.SemaphoreType.DMA((2, 3)),
        ],
        compiler_params=pltpu.CompilerParams(collective_id=0, has_side_effects=True, vmem_limit_bytes=48 * 1024 * 1024),
        cost_estimate=pl.CostEstimate(flops=10**6, bytes_accessed=4 * 10**6, transcendentals=0),
    )(halves)


def dot(a, b, contract=(1, 0)):
    return lax.dot_general(a, b, (((contract[0],), (contract[1],)), ((), ())), preferred_element_type=jnp.float32)


def centre_scale(values):
    offset = values - jnp.mean(values, axis=-1, keepdims=True)
    scale = lax.rsqrt(jnp.mean(offset * offset, axis=-1, keepdims=True) + 1e-06)
    return offset * scale, scale


def norm_back(grad, unit, scale):
    return scale * (grad - jnp.mean(grad, axis=-1, keepdims=True) - unit * jnp.mean(grad * unit, axis=-1, keepdims=True))


def gelu_rows(expand, hidden, slope, rows, columns):
    across = expand.shape[1] // columns

    def body(i, carry):
        here = pl.ds(pl.multiple_of(i * rows, rows), rows)
        for c in range(across):
            there = slice(c * columns, (c + 1) * columns)
            v = expand[here, there]
            below = 0.5 + 0.5 * lax.erf(v * 0.7071067811865476)
            hidden[here, there] = (v * below).astype(jnp.bfloat16)
            slope[here, there] = below + v * (jnp.exp(v * v * -0.5) * 0.3989422804014327)
        return carry

    lax.fori_loop(0, expand.shape[0] // rows, body, 0)


def side_sum(shifted, taps, out, flip):
    span, side = shifted.shape[0], shifted.shape[1]
    reach = span // 2
    for i in range(side):
        total = None
        for other in range(max(0, i - reach), min(side, i + reach + 1)):
            row = reach + (i - other if flip else other - i)
            for d in range(span):
                term = shifted[d, other] * taps[row, (span - 1 - d) if flip else d]
                total = term if total is None else total + term
        out[i] = total


def compute_kernel(feats, cot, keep, plan, kernel_one, gain_one, inward_one, outward_one, gain_down, project, kernel_two,
                   gain_two, inward_two, outward_two, features, halves, pad_one, shift_one, taps_one, conv_one, expand, hidden,
                   slope, pad_two, shift_two, taps_two, conv_two, rows_two, expand_two, hidden_two, slope_two):
    tiles, side, _, narrow = feats.shape
    half = side // 2
    wide = project.shape[1]
    span = kernel_one.shape[0]
    reach = span // 2
    rows, small = tiles * side * side, tiles * half * half
    f32, bf16 = jnp.float32, jnp.bfloat16
    lives = []
    for t in range(tiles):
        place = sum(jnp.where(keep[0, p] == t, p, 0) for p in range(tiles))
        lives.append(jnp.where(place < plan[0, 0], 1.0, 0.0).astype(f32))

    for d in range(span):
        taps_one[d] = jnp.broadcast_to(kernel_one[d].astype(f32)[:, None, :], (span, 8, narrow))
        taps_two[d] = jnp.broadcast_to(kernel_two[d].astype(f32)[:, None, :], (span, 8, wide))
    pad_one[...] = jnp.zeros_like(pad_one)
    for t in range(tiles):
        pad_one[:, t, 8:8 + side, :] = feats[t].astype(f32) * lives[t]
    for d in range(span):
        shift_one[d] = pad_one[:, :, 8 + d - reach:8 + d - reach + side, :]
    side_sum(shift_one, taps_one, conv_one, False)
    unit, _ = centre_scale(conv_one[...].reshape(rows, narrow))
    normed = (unit * gain_one[...].astype(f32)).astype(bf16)
    plain = pad_one[:, :, 8:8 + side, :].reshape(rows, narrow).astype(bf16)
    to = lax.broadcasted_iota(jnp.int32, (rows, rows), 0)
    column_pair, rest = to & (half - 1), to >> (half.bit_length() - 1)
    tile, rest = rest & (tiles - 1), rest >> (tiles.bit_length() - 1)
    row_pair, rest = rest & (half - 1), rest >> (half.bit_length() - 1)
    source = ((row_pair * 2 + (rest >> 1)) * tiles + tile) * side + column_pair * 2 + (rest & 1)
    order = jnp.where(lax.broadcasted_iota(jnp.int32, (rows, rows), 1) == source, 1.0, 0.0).astype(bf16)
    normed = dot(order, normed).astype(bf16)
    plain = dot(order, plain)
    expand[...] = dot(normed, inward_one[...])
    gelu_rows(expand, hidden, slope, 16, expand.shape[1])
    section = (plain + dot(hidden[...], outward_one[...])).astype(bf16).astype(f32)
    unit_down, scale_down = centre_scale(section)
    gain = gain_down[...].astype(f32)
    down = (unit_down * gain).astype(bf16)
    merged = sum(dot(down[q * small:(q + 1) * small], project[q * narrow:(q + 1) * narrow]) for q in range(4)).astype(bf16).astype(f32)

    lane = lax.broadcasted_iota(jnp.int32, (half, tiles * half, wide), 1) & (half - 1)

    def second_conv(values, flip):
        pad_two[...] = jnp.zeros_like(pad_two)
        pad_two[:, 8:8 + tiles * half, :] = values.reshape(half, tiles * half, wide)
        for d in range(span):
            at = lane + (d - reach)
            moved = pad_two[:, 8 + d - reach:8 + d - reach + tiles * half, :]
            shift_two[d] = jnp.where((at >= 0) & (at < half), moved, 0.0).reshape(half, tiles * half // 8, 8, wide)
        side_sum(shift_two, taps_two, conv_two, flip)
        return conv_two[...].reshape(small, wide)

    unit_two, scale_two = centre_scale(second_conv(merged, False))
    second_gain = gain_two[...].astype(f32)
    normed_two = (unit_two * second_gain).astype(bf16)
    expand_two[...] = dot(normed_two, inward_two[...])
    gelu_rows(expand_two, hidden_two, slope_two, 16, expand_two.shape[1] // 2)
    rows_two[...] = merged + dot(hidden_two[...], outward_two[...])
    for t in range(tiles):
        for i in range(half):
            at = (i * tiles + t) * half
            features[t, i] = (rows_two[at:at + half] * lives[t]).astype(bf16)
    for t in range(tiles):
        for i in range(half):
            at = (i * tiles + t) * half
            rows_two[at:at + half] = cot[t, i].astype(f32) * lives[t]
    cotangent = rows_two[...]
    back = dot(cotangent.astype(bf16), outward_two[...], (1, 1)).astype(bf16).astype(f32)
    back = (slope_two[...] * back).astype(bf16)
    back = dot(back, inward_two[...], (1, 1)).astype(bf16).astype(f32)
    back = second_conv(norm_back(back * second_gain, unit_two, scale_two), True)
    back_merged = (cotangent + back).astype(bf16)

    spots, line, part = halves.shape[1:4]

    def put(where, start, value):
        for at in range(0, value.shape[0], part):
            whole = (start + at) // part
            halves[where, whole % spots, whole // spots] = value[at:at + part].astype(halves.dtype)

    grad_project = jnp.concatenate([dot(down[q * small:(q + 1) * small], back_merged, (0, 0)) for q in range(4)], axis=0)
    put(0, 0, grad_project)
    back_down = jnp.concatenate([dot(back_merged, project[q * narrow:(q + 1) * narrow], (1, 1)) for q in range(4)], axis=0)
    back_down = back_down.astype(bf16).astype(f32)
    back_section = norm_back(back_down * gain, unit_down, scale_down).astype(bf16)
    grad_outward = dot(hidden[...], back_section, (0, 0))
    back_hidden = dot(back_section, outward_one[...], (1, 1)).astype(bf16).astype(f32)
    back_expand = (slope[...] * back_hidden).astype(bf16)
    grad_inward = dot(back_expand, normed, (0, 0))
    put(1, 0, jnp.concatenate([grad_inward, grad_outward], axis=1))


def compute_scratch(tiles, side, narrow, wide, span, inner, inner_two):
    half = side // 2
    rows, small = tiles * side * side, tiles * half * half
    f32, bf16 = jnp.float32, jnp.bfloat16
    return [
        pltpu.VMEM((side, tiles, side + 16, narrow), f32),
        pltpu.VMEM((span, side, tiles, side, narrow), f32),
        pltpu.VMEM((span, span, 8, narrow), f32),
        pltpu.VMEM((side, tiles, side, narrow), f32),
        pltpu.VMEM((rows, inner), f32),
        pltpu.VMEM((rows, inner), bf16),
        pltpu.VMEM((rows, inner), f32),
        pltpu.VMEM((half, tiles * half + 16, wide), f32),
        pltpu.VMEM((span, half, tiles * half // 8, 8, wide), f32),
        pltpu.VMEM((span, span, 8, wide), f32),
        pltpu.VMEM((half, tiles * half // 8, 8, wide), f32),
        pltpu.VMEM((small, wide), f32),
        pltpu.VMEM((small, inner_two), f32),
        pltpu.VMEM((small, inner_two), bf16),
        pltpu.VMEM((small, inner_two), f32),
    ]


def fits(slides, reps, rows):
    return reps == 4 and slides % 2 == 0 and slides > 2 and rows % (slides * 32) == 0


def per_device(tile_feats, cotangent, keep_list, tile_plan, kernel_one, gain_one, inward_one, outward_one, gain_down,
               project_down, kernel_two, gain_two, inward_two, outward_two):
    slides, reps = lax.axis_size("slide"), lax.axis_size("rep")
    rows, wide = project_down.shape
    narrow = tile_feats.shape[3]
    direct = fits(slides, reps, rows)
    cut = (4, slides // 2, rows // slides // 2) if direct else (1, 1, rows)
    whole = pl.BlockSpec(memory_space=pltpu.VMEM)
    scalars = pl.BlockSpec(memory_space=pltpu.SMEM)
    features, halves = pl.pallas_call(
        compute_kernel,
        out_shape=(
            jax.ShapeDtypeStruct(cotangent.shape, jnp.bfloat16),
            jax.ShapeDtypeStruct((2,) + cut + (wide,), jnp.bfloat16 if direct else jnp.float32),
        ),
        in_specs=[whole, whole, scalars, scalars] + [whole] * 10,
        out_specs=(whole, whole),
        scratch_shapes=compute_scratch(
            tile_feats.shape[0], tile_feats.shape[1], narrow, wide, kernel_one.shape[0], inward_one.shape[1], inward_two.shape[1]),
        compiler_params=pltpu.CompilerParams(vmem_limit_bytes=48 * 1024 * 1024),
    )(tile_feats, cotangent, keep_list, tile_plan, kernel_one, gain_one[None], inward_one, outward_one, gain_down[None],
      project_down, kernel_two, gain_two[None], inward_two, outward_two)
    if direct:
        got = exchange(halves, slides).reshape(2, rows // slides, wide)
        project, both = got[0], got[1]
    else:
        project, both = (
            lax.psum(lax.psum_scatter(g.reshape(rows, wide), "slide", scatter_dimension=0, tiled=True), "rep")
            for g in (halves[0], halves[1]))
    return features, both[:, :narrow].T, both[:, narrow:], project


def solution(mesh):
    in_specs = (
        P(("slide", "rep"), None, None, None),
        P(("slide", "rep"), None, None, None),
        P(("slide", "rep"), None),
        P(("slide", "rep"), None),
        P(),
        P(),
        P(),
        P(),
        P(),
        P(),
        P(),
        P(),
        P(),
        P(),
    )
    out_specs = (
        P(("slide", "rep"), None, None, None),
        P(None, "slide"),
        P("slide", None),
        P("slide", None),
    )
    return jax.shard_map(
        per_device, mesh=mesh, in_specs=in_specs, out_specs=out_specs, check_vma=False
    )
```

```python
import functools

import jax
import jax.numpy as jnp
from jax import lax
from jax.experimental import pallas as pl
from jax.experimental.pallas import tpu as pltpu
from jax.sharding import PartitionSpec as P

MESH = pl.DeviceIdType.MESH


def exchange_kernel(line, halves, out, get_pair, put_quad, get_quad, mine, put_line, get_line, put_rep, get_rep, pair_sems, quad_sems, line_sems, rep_sems):
    s = lax.axis_index("slide")
    r = lax.axis_index("rep")
    core, y = r % 2, r // 2
    x, z = s % 2, s // 2
    spot = x * 2 + y
    pair_peer = (s, y * 2 + 1 - core)

    def quad_peer(d):
        return (z * 2 + (x + d // 2) % 2, ((y + d) % 2) * 2 + core)

    def line_peer(d):
        return (((z + d) % line) * 2 + x, r)

    def rep_peer(d):
        return (s, ((y + d // 2) % 2) * 2 + (core + d) % 2)

    def quad_spot(d):
        return ((x + d // 2) % 2) * 2 + (y + d) % 2

    barrier = pltpu.get_barrier_semaphore()
    peers = [rep_peer(d) for d in (1, 2, 3)] + [quad_peer(d) for d in (2, 3)] + [line_peer(d) for d in range(1, line)]
    for peer in peers:
        pl.semaphore_signal(barrier, inc=1, device_id=peer, device_id_type=MESH)
    pl.semaphore_wait(barrier, len(peers))

    def send(src, dst, sems, slot, peer):
        copy = pltpu.make_async_remote_copy(
            src_ref=src, dst_ref=dst, send_sem=sems.at[0, slot], recv_sem=sems.at[1, slot],
            device_id=peer, device_id_type=MESH)
        copy.start()
        return copy

    pairs = {}
    for d in (3, 2, 1, 0):
        pairs[d] = send(halves.at[1 - core, quad_spot(d)], get_pair.at[d], pair_sems, d, pair_peer)
    quads = {}
    for d in (3, 2, 1):
        pairs[d].wait_recv()
        put_quad[d - 1] = (halves[core, quad_spot(d)].astype(jnp.float32) + get_pair[d].astype(jnp.float32)).astype(jnp.bfloat16)
        quads[d] = send(put_quad.at[d - 1], get_quad.at[d - 1], quad_sems, d - 1, quad_peer(d))
    pairs[0].wait_recv()
    mine[...] = halves[core, spot].astype(jnp.float32) + get_pair[0].astype(jnp.float32)
    for d in (1, 2, 3):
        quads[d].wait_recv()
    lines = {}
    for d in [*range(line - 1, 0, -1), 0]:
        at = (z + d) % line
        part = mine[at] + get_quad[0, at].astype(jnp.float32) + get_quad[1, at].astype(jnp.float32) + get_quad[2, at].astype(jnp.float32)
        if d:
            put_line[d - 1] = part.astype(jnp.bfloat16)
            lines[d] = send(put_line.at[d - 1], get_line.at[d - 1], line_sems, d - 1, line_peer(d))
        else:
            total = part
    for d in range(1, line):
        lines[d].wait_recv()
        total = total + get_line[d - 1].astype(jnp.float32)
    put_rep[...] = total.astype(jnp.bfloat16)
    reps = {}
    for d in (3, 2, 1):
        reps[d] = send(put_rep, get_rep.at[d - 1], rep_sems, d - 1, rep_peer(d))
    out[core, y] = put_rep[...]
    for d in (1, 3, 2):
        reps[d].wait_recv()
        out[(core + d) % 2, (y + d // 2) % 2] = get_rep[d - 1]
    for copy in [*pairs.values(), *quads.values(), *lines.values(), *reps.values()]:
        copy.wait_send()


def exchange(halves, slides):
    line = slides // 2
    block = halves.shape[-2:]
    return pl.pallas_call(
        functools.partial(exchange_kernel, line),
        out_shape=jax.ShapeDtypeStruct((2, 2) + block, jnp.bfloat16),
        in_specs=[pl.BlockSpec(memory_space=pltpu.VMEM)],
        out_specs=pl.BlockSpec(memory_space=pltpu.VMEM),
        scratch_shapes=[
            pltpu.VMEM((4, line) + block, jnp.bfloat16),
            pltpu.VMEM((3, line) + block, jnp.bfloat16),
            pltpu.VMEM((3, line) + block, jnp.bfloat16),
            pltpu.VMEM((line,) + block, jnp.float32),
            pltpu.VMEM((line - 1,) + block, jnp.bfloat16),
            pltpu.VMEM((line - 1,) + block, jnp.bfloat16),
            pltpu.VMEM(block, jnp.bfloat16),
            pltpu.VMEM((3,) + block, jnp.bfloat16),
            pltpu.SemaphoreType.DMA((2, 4)),
            pltpu.SemaphoreType.DMA((2, 3)),
            pltpu.SemaphoreType.DMA((2, line - 1)),
            pltpu.SemaphoreType.DMA((2, 3)),
        ],
        compiler_params=pltpu.CompilerParams(collective_id=0, has_side_effects=True, vmem_limit_bytes=48 * 1024 * 1024),
        cost_estimate=pl.CostEstimate(flops=10**6, bytes_accessed=4 * 10**6, transcendentals=0),
    )(halves)


def dot(a, b, contract=(1, 0)):
    return lax.dot_general(a, b, (((contract[0],), (contract[1],)), ((), ())), preferred_element_type=jnp.float32)


def centre_scale(values):
    offset = values - jnp.mean(values, axis=-1, keepdims=True)
    scale = lax.rsqrt(jnp.mean(offset * offset, axis=-1, keepdims=True) + 1e-06)
    return offset * scale, scale


def norm_back(grad, unit, scale):
    return scale * (grad - jnp.mean(grad, axis=-1, keepdims=True) - unit * jnp.mean(grad * unit, axis=-1, keepdims=True))


def gelu_rows(expand, hidden, slope, rows, columns):
    across = expand.shape[1] // columns

    def body(i, carry):
        here = pl.ds(pl.multiple_of(i * rows, rows), rows)
        for c in range(across):
            there = slice(c * columns, (c + 1) * columns)
            v = expand[here, there]
            below = 0.5 + 0.5 * lax.erf(v * 0.7071067811865476)
            hidden[here, there] = (v * below).astype(jnp.bfloat16)
            slope[here, there] = below + v * (jnp.exp(v * v * -0.5) * 0.3989422804014327)
        return carry

    lax.fori_loop(0, expand.shape[0] // rows, body, 0)


def side_sum(shifted, taps, out, flip):
    span, side = shifted.shape[0], shifted.shape[1]
    reach = span // 2
    for i in range(side):
        total = None
        for other in range(max(0, i - reach), min(side, i + reach + 1)):
            row = reach + (i - other if flip else other - i)
            for d in range(span):
                term = shifted[d, other] * taps[row, (span - 1 - d) if flip else d]
                total = term if total is None else total + term
        out[i] = total


def compute_kernel(*refs):
    count = 14
    far, features, halves = refs[:count], refs[count], refs[count + 1]
    near, sems = refs[count + 2:2 * count + 2], refs[2 * count + 2]
    fetches = [pltpu.make_async_copy(far[i], near[i], sems.at[i]) for i in range(count)]
    for i in (2, 3, 0, 4, 5, 6, 7, 8, 9, 10, 11, 12, 1, 13):
        fetches[i].start()
    step(*near, features, halves, *refs[2 * count + 3:], fetches)


def step(feats, cot, keep, plan, kernel_one, gain_one, inward_one, outward_one, gain_down, project, kernel_two,
         gain_two, inward_two, outward_two, features, halves, pad_one, shift_one, taps_one, conv_one, expand, hidden,
                   slope, pad_two, shift_two, taps_two, conv_two, rows_two, expand_two, hidden_two, slope_two, fetches):
    tiles, side, _, narrow = feats.shape
    half = side // 2
    wide = project.shape[1]
    span = kernel_one.shape[0]
    reach = span // 2
    rows, small = tiles * side * side, tiles * half * half
    f32, bf16 = jnp.float32, jnp.bfloat16
    def arrive(*which):
        for i in which:
            fetches[i].wait()

    arrive(2, 3)
    lives = []
    for t in range(tiles):
        place = sum(jnp.where(keep[0, p] == t, p, 0) for p in range(tiles))
        lives.append(jnp.where(place < plan[0, 0], 1.0, 0.0).astype(f32))

    arrive(0, 4)
    for d in range(span):
        taps_one[d] = jnp.broadcast_to(kernel_one[d].astype(f32)[:, None, :], (span, 8, narrow))
    pad_one[...] = jnp.zeros_like(pad_one)
    for t in range(tiles):
        pad_one[:, t, 8:8 + side, :] = feats[t].astype(f32) * lives[t]
    for d in range(span):
        shift_one[d] = pad_one[:, :, 8 + d - reach:8 + d - reach + side, :]
    side_sum(shift_one, taps_one, conv_one, False)
    arrive(5, 6, 7)
    unit, _ = centre_scale(conv_one[...].reshape(rows, narrow))
    normed = (unit * gain_one[...].astype(f32)[None]).astype(bf16)
    plain = pad_one[:, :, 8:8 + side, :].reshape(rows, narrow).astype(bf16)
    to = lax.broadcasted_iota(jnp.int32, (rows, rows), 0)
    column_pair, rest = to & (half - 1), to >> (half.bit_length() - 1)
    tile, rest = rest & (tiles - 1), rest >> (tiles.bit_length() - 1)
    row_pair, rest = rest & (half - 1), rest >> (half.bit_length() - 1)
    source = ((row_pair * 2 + (rest >> 1)) * tiles + tile) * side + column_pair * 2 + (rest & 1)
    order = jnp.where(lax.broadcasted_iota(jnp.int32, (rows, rows), 1) == source, 1.0, 0.0).astype(bf16)
    normed = dot(order, normed).astype(bf16)
    plain = dot(order, plain)
    expand[...] = dot(normed, inward_one[...])
    gelu_rows(expand, hidden, slope, 16, expand.shape[1])
    arrive(8, 9, 10, 11, 12, 1, 13)
    section = (plain + dot(hidden[...], outward_one[...], (1, 1))).astype(bf16).astype(f32)
    unit_down, scale_down = centre_scale(section)
    gain = gain_down[...].astype(f32)[None]
    down = (unit_down * gain).astype(bf16)
    merged = sum(dot(down[q * small:(q + 1) * small], project[q * narrow:(q + 1) * narrow]) for q in range(4)).astype(bf16).astype(f32)

    for d in range(span):
        taps_two[d] = jnp.broadcast_to(kernel_two[d].astype(f32)[:, None, :], (span, 8, wide))
    lane = lax.broadcasted_iota(jnp.int32, (half, tiles * half, wide), 1) & (half - 1)

    def second_conv(values, flip):
        pad_two[...] = jnp.zeros_like(pad_two)
        pad_two[:, 8:8 + tiles * half, :] = values.reshape(half, tiles * half, wide)
        for d in range(span):
            at = lane + (d - reach)
            moved = pad_two[:, 8 + d - reach:8 + d - reach + tiles * half, :]
            shift_two[d] = jnp.where((at >= 0) & (at < half), moved, 0.0).reshape(half, tiles * half // 8, 8, wide)
        side_sum(shift_two, taps_two, conv_two, flip)
        return conv_two[...].reshape(small, wide)

    unit_two, scale_two = centre_scale(second_conv(merged, False))
    second_gain = gain_two[...].astype(f32)[None]
    normed_two = (unit_two * second_gain).astype(bf16)
    expand_two[...] = dot(normed_two, inward_two[...])
    gelu_rows(expand_two, hidden_two, slope_two, 16, expand_two.shape[1] // 2)
    rows_two[...] = merged + dot(hidden_two[...], outward_two[...])
    for t in range(tiles):
        for i in range(half):
            at = (i * tiles + t) * half
            features[t, i] = (rows_two[at:at + half] * lives[t]).astype(bf16)
    for t in range(tiles):
        for i in range(half):
            at = (i * tiles + t) * half
            rows_two[at:at + half] = cot[t, i].astype(f32) * lives[t]
    cotangent = rows_two[...]
    back = dot(cotangent.astype(bf16), outward_two[...], (1, 1)).astype(bf16).astype(f32)
    back = (slope_two[...] * back).astype(bf16)
    back = dot(back, inward_two[...], (1, 1)).astype(bf16).astype(f32)
    back = second_conv(norm_back(back * second_gain, unit_two, scale_two), True)
    back_merged = (cotangent + back).astype(bf16)

    spots, line, part = halves.shape[1:4]

    def put(where, start, value):
        for at in range(0, value.shape[0], part):
            whole = (start + at) // part
            halves[where, whole % spots, whole // spots] = value[at:at + part].astype(halves.dtype)

    grad_project = jnp.concatenate([dot(down[q * small:(q + 1) * small], back_merged, (0, 0)) for q in range(4)], axis=0)
    put(0, 0, grad_project)
    back_down = jnp.concatenate([dot(back_merged, project[q * narrow:(q + 1) * narrow], (1, 1)) for q in range(4)], axis=0)
    back_down = back_down.astype(bf16).astype(f32)
    back_section = norm_back(back_down * gain, unit_down, scale_down).astype(bf16)
    grad_outward = dot(hidden[...], back_section, (0, 0))
    back_hidden = dot(back_section, outward_one[...]).astype(bf16).astype(f32)
    back_expand = (slope[...] * back_hidden).astype(bf16)
    grad_inward = dot(back_expand, normed, (0, 0))
    put(1, 0, jnp.concatenate([grad_inward, grad_outward], axis=1))


def compute_scratch(tiles, side, narrow, wide, span, inner, inner_two):
    half = side // 2
    rows, small = tiles * side * side, tiles * half * half
    f32, bf16 = jnp.float32, jnp.bfloat16
    return [
        pltpu.VMEM((side, tiles, side + 16, narrow), f32),
        pltpu.VMEM((span, side, tiles, side, narrow), f32),
        pltpu.VMEM((span, span, 8, narrow), f32),
        pltpu.VMEM((side, tiles, side, narrow), f32),
        pltpu.VMEM((rows, inner), f32),
        pltpu.VMEM((rows, inner), bf16),
        pltpu.VMEM((rows, inner), f32),
        pltpu.VMEM((half, tiles * half + 16, wide), f32),
        pltpu.VMEM((span, half, tiles * half // 8, 8, wide), f32),
        pltpu.VMEM((span, span, 8, wide), f32),
        pltpu.VMEM((half, tiles * half // 8, 8, wide), f32),
        pltpu.VMEM((small, wide), f32),
        pltpu.VMEM((small, inner_two), f32),
        pltpu.VMEM((small, inner_two), bf16),
        pltpu.VMEM((small, inner_two), f32),
    ]


def finish_kernel(got, inward, outward, project):
    part, narrow = got.shape[2], outward.shape[1]
    both = jnp.concatenate([got[1, y].astype(jnp.float32) for y in range(2)], axis=0)
    inward[...] = both[:, :narrow].T
    outward[...] = both[:, narrow:]
    for y in range(2):
        project[y * part:(y + 1) * part] = got[0, y].astype(jnp.float32)


def fits(slides, reps, rows):
    return reps == 4 and slides % 2 == 0 and slides > 2 and rows % (slides * 32) == 0


def per_device(tile_feats, cotangent, keep_list, tile_plan, kernel_one, gain_one, inward_one, outward_one, gain_down,
               project_down, kernel_two, gain_two, inward_two, outward_two):
    slides, reps = lax.axis_size("slide"), lax.axis_size("rep")
    rows, wide = project_down.shape
    narrow = tile_feats.shape[3]
    direct = fits(slides, reps, rows)
    cut = (4, slides // 2, rows // slides // 2) if direct else (1, 1, rows)
    operands = (tile_feats, cotangent, keep_list, tile_plan, kernel_one, gain_one, inward_one, outward_one.T, gain_down,
                project_down, kernel_two, gain_two, inward_two, outward_two)
    spaces = [pltpu.SMEM if a.dtype == jnp.int32 else pltpu.VMEM for a in operands]
    whole = pl.BlockSpec(memory_space=pltpu.VMEM)
    features, halves = pl.pallas_call(
        compute_kernel,
        out_shape=(
            jax.ShapeDtypeStruct(cotangent.shape, jnp.bfloat16),
            jax.ShapeDtypeStruct((2,) + cut + (wide,), jnp.bfloat16 if direct else jnp.float32),
        ),
        in_specs=[pl.BlockSpec(memory_space=pltpu.HBM)] * len(operands),
        out_specs=(whole, whole),
        scratch_shapes=[space(a.shape, a.dtype) for space, a in zip(spaces, operands)]
        + [pltpu.SemaphoreType.DMA((len(operands),))]
        + compute_scratch(
            tile_feats.shape[0], tile_feats.shape[1], narrow, wide, kernel_one.shape[0], inward_one.shape[1], inward_two.shape[1]),
        compiler_params=pltpu.CompilerParams(vmem_limit_bytes=60 * 1024 * 1024),
    )(*operands)
    if not direct:
        project, both = (
            lax.psum(lax.psum_scatter(g.reshape(rows, wide), "slide", scatter_dimension=0, tiled=True), "rep")
            for g in (halves[0], halves[1]))
        return features, both[:, :narrow].T, both[:, narrow:], project
    share = rows // slides
    inward, outward, project = pl.pallas_call(
        finish_kernel,
        out_shape=tuple(jax.ShapeDtypeStruct(d, jnp.float32) for d in ((narrow, share), (share, narrow), (share, wide))),
        in_specs=[whole],
        out_specs=(whole,) * 3,
    )(exchange(halves, slides))
    return features, inward, outward, project


def solution(mesh):
    in_specs = (
        P(("slide", "rep"), None, None, None),
        P(("slide", "rep"), None, None, None),
        P(("slide", "rep"), None),
        P(("slide", "rep"), None),
        P(),
        P(),
        P(),
        P(),
        P(),
        P(),
        P(),
        P(),
        P(),
        P(),
    )
    out_specs = (
        P(("slide", "rep"), None, None, None),
        P(None, "slide"),
        P("slide", None),
        P("slide", None),
    )
    return jax.shard_map(
        per_device, mesh=mesh, in_specs=in_specs, out_specs=out_specs, check_vma=False
    )
```

```python
import functools

import jax
import jax.numpy as jnp
from jax import lax
from jax.experimental import pallas as pl
from jax.experimental.pallas import tpu as pltpu
from jax.sharding import PartitionSpec as P

MESH = pl.DeviceIdType.MESH


def exchange_kernel(line, halves, out, own, get_pair, put_sq, get_sq, put_ln, get_ln, mine_a, mine_b, put_a, get_a, put_b, get_b,
                    put_rep, get_rep, own_sem, pair_sems, sq_sems, ln_sems, a_sems, b_sems, rep_sems):
    s = lax.axis_index("slide")
    r = lax.axis_index("rep")
    core, y = r % 2, r // 2
    x, z = s % 2, s // 2
    cut = put_sq.shape[-1]
    pair_peer = (s, y * 2 + 1 - core)
    own_copy = pltpu.make_async_copy(halves.at[core], own, own_sem)
    own_copy.start()

    def quad_peer(d):
        return (z * 2 + (x + d // 2) % 2, ((y + d) % 2) * 2 + core)

    def line_peer(d):
        return (((z + d) % line) * 2 + x, r)

    def rep_peer(d):
        return (s, ((y + d // 2) % 2) * 2 + (core + d) % 2)

    def quad_spot(d):
        return ((x + d // 2) % 2) * 2 + (y + d) % 2

    barrier = pltpu.get_barrier_semaphore()
    peers = [rep_peer(d) for d in (1, 2, 3)] + [quad_peer(d) for d in (2, 3)] + [line_peer(d) for d in range(1, line)]
    for peer in peers:
        pl.semaphore_signal(barrier, inc=1, device_id=peer, device_id_type=MESH)
    pl.semaphore_wait(barrier, len(peers))
    started = []

    def send(src, dst, sems, slot, peer):
        copy = pltpu.make_async_remote_copy(
            src_ref=src, dst_ref=dst, send_sem=sems.at[0, slot], recv_sem=sems.at[1, slot],
            device_id=peer, device_id_type=MESH)
        copy.start()
        started.append(copy)
        return copy

    def wide(value):
        return value.astype(jnp.float32)

    others = range(line - 1, 0, -1)
    pairs = {d: send(halves.at[1 - core, quad_spot(d)], get_pair.at[d], pair_sems, d, pair_peer) for d in (3, 2, 1, 0)}
    own_copy.wait()
    squares, lines = {}, {}
    for d in (3, 2, 1, 0):
        pairs[d].wait_recv()
        q = quad_spot(d)
        first = wide(own[q, :, :, :cut]) + wide(get_pair[d, :, :, :cut])
        if d:
            put_sq[d - 1] = first.astype(jnp.bfloat16)
            squares[d] = send(put_sq.at[d - 1], get_sq.at[d - 1], sq_sems, d - 1, quad_peer(d))
        else:
            mine_a[...] = first
        for e in (*others, 0):
            at = (z + e) % line
            last = wide(own[q, at, :, cut:]) + wide(get_pair[d, at, :, cut:])
            if e:
                put_ln[e - 1, q] = last.astype(jnp.bfloat16)
            else:
                mine_b[q] = last
    for e in others:
        lines[e] = send(put_ln.at[e - 1], get_ln.at[e - 1], ln_sems, e - 1, line_peer(e))
    for d in squares:
        squares[d].wait_recv()
    then = []
    for e in (*others, 0):
        at = (z + e) % line
        total_a = mine_a[at] + wide(get_sq[0, at]) + wide(get_sq[1, at]) + wide(get_sq[2, at])
        if e:
            put_a[e - 1] = total_a.astype(jnp.bfloat16)
            then.append(send(put_a.at[e - 1], get_a.at[e - 1], a_sems, e - 1, line_peer(e)))
    for e in lines:
        lines[e].wait_recv()
    for d in (3, 2, 1, 0):
        q = quad_spot(d)
        total_b = mine_b[q]
        for e in others:
            total_b = total_b + wide(get_ln[e - 1, q])
        if d:
            put_b[d - 1] = total_b.astype(jnp.bfloat16)
            then.append(send(put_b.at[d - 1], get_b.at[d - 1], b_sems, d - 1, quad_peer(d)))
    for copy in then:
        copy.wait_recv()
    for e in others:
        total_a = total_a + wide(get_a[e - 1])
    for d in (1, 2, 3):
        total_b = total_b + wide(get_b[d - 1])
    put_rep[:, :cut] = total_a.astype(jnp.bfloat16)
    put_rep[:, cut:] = total_b.astype(jnp.bfloat16)
    reps = {d: send(put_rep, get_rep.at[d - 1], rep_sems, d - 1, rep_peer(d)) for d in (3, 2, 1)}
    out[core, y] = put_rep[...]
    for d in (1, 3, 2):
        reps[d].wait_recv()
        out[(core + d) % 2, (y + d // 2) % 2] = get_rep[d - 1]
    for copy in started:
        copy.wait_send()


def exchange(halves, slides):
    line = slides // 2
    part, width = halves.shape[-2:]
    cut = width // 3 * 2
    first, last, block = (part, cut), (part, width - cut), (part, width)
    bf16, f32 = jnp.bfloat16, jnp.float32
    buffers = [
        ((4, line) + block, bf16), ((4, line) + block, bf16),
        ((3, line) + first, bf16), ((3, line) + first, bf16),
        ((line - 1, 4) + last, bf16), ((line - 1, 4) + last, bf16),
        ((line,) + first, f32), ((4,) + last, f32),
        ((line - 1,) + first, bf16), ((line - 1,) + first, bf16),
        ((3,) + last, bf16), ((3,) + last, bf16),
        (block, bf16), ((3,) + block, bf16),
    ]
    slots = (4, 3, line - 1, line - 1, 3, 3)
    return pl.pallas_call(
        functools.partial(exchange_kernel, line),
        out_shape=jax.ShapeDtypeStruct((2, 2) + block, bf16),
        in_specs=[pl.BlockSpec(memory_space=pl.ANY)],
        out_specs=pl.BlockSpec(memory_space=pltpu.VMEM),
        scratch_shapes=[pltpu.VMEM(*b) for b in buffers]
        + [pltpu.SemaphoreType.DMA] + [pltpu.SemaphoreType.DMA((2, n)) for n in slots],
        compiler_params=pltpu.CompilerParams(collective_id=0, has_side_effects=True, vmem_limit_bytes=60 * 1024 * 1024),
        cost_estimate=pl.CostEstimate(flops=10**6, bytes_accessed=4 * 10**6, transcendentals=0),
    )(halves)


def dot(a, b, contract=(1, 0)):
    return lax.dot_general(a, b, (((contract[0],), (contract[1],)), ((), ())), preferred_element_type=jnp.float32)


def centre_scale(values):
    offset = values - jnp.mean(values, axis=-1, keepdims=True)
    scale = lax.rsqrt(jnp.mean(offset * offset, axis=-1, keepdims=True) + 1e-06)
    return offset * scale, scale


def norm_back(grad, unit, scale):
    return scale * (grad - jnp.mean(grad, axis=-1, keepdims=True) - unit * jnp.mean(grad * unit, axis=-1, keepdims=True))


def gelu_rows(expand, hidden, slope, rows, columns):
    across = expand.shape[1] // columns

    def body(i, carry):
        here = pl.ds(pl.multiple_of(i * rows, rows), rows)
        for c in range(across):
            there = slice(c * columns, (c + 1) * columns)
            v = expand[here, there]
            below = 0.5 + 0.5 * lax.erf(v * 0.7071067811865476)
            hidden[here, there] = (v * below).astype(jnp.bfloat16)
            slope[here, there] = below + v * (jnp.exp(v * v * -0.5) * 0.3989422804014327)
        return carry

    lax.fori_loop(0, expand.shape[0] // rows, body, 0)


def side_sum(shifted, taps, out, flip):
    span, side = shifted.shape[0], shifted.shape[1]
    reach = span // 2
    for i in range(side):
        total = None
        for other in range(max(0, i - reach), min(side, i + reach + 1)):
            row = reach + (i - other if flip else other - i)
            for d in range(span):
                term = shifted[d, other] * taps[row, (span - 1 - d) if flip else d]
                total = term if total is None else total + term
        out[i] = total


def compute_kernel(*refs):
    count = 14
    far, features, halves = refs[:count], refs[count], refs[count + 1]
    near, sems = refs[count + 2:2 * count + 2], refs[2 * count + 2]
    fetches = [pltpu.make_async_copy(far[i], near[i], sems.at[i]) for i in range(count)]
    for i in (2, 3, 0, 4, 5, 6, 7, 8, 9, 10, 11, 12, 1, 13):
        fetches[i].start()
    step(*near, features, halves, *refs[2 * count + 3:], fetches)


def step(feats, cot, keep, plan, kernel_one, gain_one, inward_one, outward_one, gain_down, project, kernel_two,
         gain_two, inward_two, outward_two, features, halves, pad_one, shift_one, taps_one, conv_one, expand, hidden,
                   slope, pad_two, shift_two, taps_two, conv_two, rows_two, expand_two, hidden_two, slope_two, fetches):
    tiles, side, _, narrow = feats.shape
    half = side // 2
    wide = project.shape[1]
    span = kernel_one.shape[0]
    reach = span // 2
    rows, small = tiles * side * side, tiles * half * half
    f32, bf16 = jnp.float32, jnp.bfloat16
    def arrive(*which):
        for i in which:
            fetches[i].wait()

    arrive(2, 3)
    lives = []
    for t in range(tiles):
        place = sum(jnp.where(keep[0, p] == t, p, 0) for p in range(tiles))
        lives.append(jnp.where(place < plan[0, 0], 1.0, 0.0).astype(f32))

    arrive(0, 4)
    for d in range(span):
        taps_one[d] = jnp.broadcast_to(kernel_one[d].astype(f32)[:, None, :], (span, 8, narrow))
    pad_one[...] = jnp.zeros_like(pad_one)
    for t in range(tiles):
        pad_one[:, t, 8:8 + side, :] = feats[t].astype(f32) * lives[t]
    for d in range(span):
        shift_one[d] = pad_one[:, :, 8 + d - reach:8 + d - reach + side, :]
    side_sum(shift_one, taps_one, conv_one, False)
    arrive(5, 6, 7)
    unit, _ = centre_scale(conv_one[...].reshape(rows, narrow))
    normed = (unit * gain_one[...].astype(f32)[None]).astype(bf16)
    plain = pad_one[:, :, 8:8 + side, :].reshape(rows, narrow).astype(bf16)
    to = lax.broadcasted_iota(jnp.int32, (rows, rows), 0)
    column_pair, rest = to & (half - 1), to >> (half.bit_length() - 1)
    tile, rest = rest & (tiles - 1), rest >> (tiles.bit_length() - 1)
    row_pair, rest = rest & (half - 1), rest >> (half.bit_length() - 1)
    source = ((row_pair * 2 + (rest >> 1)) * tiles + tile) * side + column_pair * 2 + (rest & 1)
    order = jnp.where(lax.broadcasted_iota(jnp.int32, (rows, rows), 1) == source, 1.0, 0.0).astype(bf16)
    normed = dot(order, normed).astype(bf16)
    plain = dot(order, plain)
    expand[...] = dot(normed, inward_one[...])
    gelu_rows(expand, hidden, slope, 16, expand.shape[1])
    arrive(8, 9, 10, 11, 12, 1, 13)
    section = (plain + dot(hidden[...], outward_one[...], (1, 1))).astype(bf16).astype(f32)
    unit_down, scale_down = centre_scale(section)
    gain = gain_down[...].astype(f32)[None]
    down = (unit_down * gain).astype(bf16)
    merged = sum(dot(down[q * small:(q + 1) * small], project[q * narrow:(q + 1) * narrow]) for q in range(4)).astype(bf16).astype(f32)

    for d in range(span):
        taps_two[d] = jnp.broadcast_to(kernel_two[d].astype(f32)[:, None, :], (span, 8, wide))
    lane = lax.broadcasted_iota(jnp.int32, (half, tiles * half, wide), 1) & (half - 1)

    def second_conv(values, flip):
        pad_two[...] = jnp.zeros_like(pad_two)
        pad_two[:, 8:8 + tiles * half, :] = values.reshape(half, tiles * half, wide)
        for d in range(span):
            at = lane + (d - reach)
            moved = pad_two[:, 8 + d - reach:8 + d - reach + tiles * half, :]
            shift_two[d] = jnp.where((at >= 0) & (at < half), moved, 0.0).reshape(half, tiles * half // 8, 8, wide)
        side_sum(shift_two, taps_two, conv_two, flip)
        return conv_two[...].reshape(small, wide)

    unit_two, scale_two = centre_scale(second_conv(merged, False))
    second_gain = gain_two[...].astype(f32)[None]
    normed_two = (unit_two * second_gain).astype(bf16)
    expand_two[...] = dot(normed_two, inward_two[...])
    gelu_rows(expand_two, hidden_two, slope_two, 16, expand_two.shape[1] // 2)
    rows_two[...] = merged + dot(hidden_two[...], outward_two[...])
    for t in range(tiles):
        for i in range(half):
            at = (i * tiles + t) * half
            features[t, i] = (rows_two[at:at + half] * lives[t]).astype(bf16)
    for t in range(tiles):
        for i in range(half):
            at = (i * tiles + t) * half
            rows_two[at:at + half] = cot[t, i].astype(f32) * lives[t]
    cotangent = rows_two[...]
    back = dot(cotangent.astype(bf16), outward_two[...], (1, 1)).astype(bf16).astype(f32)
    back = (slope_two[...] * back).astype(bf16)
    back = dot(back, inward_two[...], (1, 1)).astype(bf16).astype(f32)
    back = second_conv(norm_back(back * second_gain, unit_two, scale_two), True)
    back_merged = (cotangent + back).astype(bf16)

    spots, line, part = halves.shape[1:4]

    def put(where, start, value):
        for at in range(0, value.shape[0], part):
            whole = (start + at) // part
            halves[where, whole % spots, whole // spots] = value[at:at + part].astype(halves.dtype)

    grad_project = jnp.concatenate([dot(down[q * small:(q + 1) * small], back_merged, (0, 0)) for q in range(4)], axis=0)
    put(0, 0, grad_project)
    back_down = jnp.concatenate([dot(back_merged, project[q * narrow:(q + 1) * narrow], (1, 1)) for q in range(4)], axis=0)
    back_down = back_down.astype(bf16).astype(f32)
    back_section = norm_back(back_down * gain, unit_down, scale_down).astype(bf16)
    grad_outward = dot(hidden[...], back_section, (0, 0))
    back_hidden = dot(back_section, outward_one[...]).astype(bf16).astype(f32)
    back_expand = (slope[...] * back_hidden).astype(bf16)
    grad_inward = dot(back_expand, normed, (0, 0))
    put(1, 0, jnp.concatenate([grad_inward, grad_outward], axis=1))


def compute_scratch(tiles, side, narrow, wide, span, inner, inner_two):
    half = side // 2
    rows, small = tiles * side * side, tiles * half * half
    f32, bf16 = jnp.float32, jnp.bfloat16
    return [
        pltpu.VMEM((side, tiles, side + 16, narrow), f32),
        pltpu.VMEM((span, side, tiles, side, narrow), f32),
        pltpu.VMEM((span, span, 8, narrow), f32),
        pltpu.VMEM((side, tiles, side, narrow), f32),
        pltpu.VMEM((rows, inner), f32),
        pltpu.VMEM((rows, inner), bf16),
        pltpu.VMEM((rows, inner), f32),
        pltpu.VMEM((half, tiles * half + 16, wide), f32),
        pltpu.VMEM((span, half, tiles * half // 8, 8, wide), f32),
        pltpu.VMEM((span, span, 8, wide), f32),
        pltpu.VMEM((half, tiles * half // 8, 8, wide), f32),
        pltpu.VMEM((small, wide), f32),
        pltpu.VMEM((small, inner_two), f32),
        pltpu.VMEM((small, inner_two), bf16),
        pltpu.VMEM((small, inner_two), f32),
    ]


def finish_kernel(got, inward, outward, project):
    part, narrow = got.shape[2], outward.shape[1]
    both = jnp.concatenate([got[1, y].astype(jnp.float32) for y in range(2)], axis=0)
    inward[...] = both[:, :narrow].T
    outward[...] = both[:, narrow:]
    for y in range(2):
        project[y * part:(y + 1) * part] = got[0, y].astype(jnp.float32)


def fits(slides, reps, rows, wide):
    return wide % 384 == 0 and reps == 4 and slides % 2 == 0 and slides > 2 and rows % (slides * 32) == 0


def per_device(tile_feats, cotangent, keep_list, tile_plan, kernel_one, gain_one, inward_one, outward_one, gain_down,
               project_down, kernel_two, gain_two, inward_two, outward_two):
    slides, reps = lax.axis_size("slide"), lax.axis_size("rep")
    rows, wide = project_down.shape
    narrow = tile_feats.shape[3]
    direct = fits(slides, reps, rows, wide)
    cut = (4, slides // 2, rows // slides // 2) if direct else (1, 1, rows)
    operands = (tile_feats, cotangent, keep_list, tile_plan, kernel_one, gain_one, inward_one, outward_one.T, gain_down,
                project_down, kernel_two, gain_two, inward_two, outward_two)
    spaces = [pltpu.SMEM if a.dtype == jnp.int32 else pltpu.VMEM for a in operands]
    whole = pl.BlockSpec(memory_space=pltpu.VMEM)
    features, halves = pl.pallas_call(
        compute_kernel,
        out_shape=(
            jax.ShapeDtypeStruct(cotangent.shape, jnp.bfloat16),
            jax.ShapeDtypeStruct((2,) + cut + (wide,), jnp.bfloat16 if direct else jnp.float32),
        ),
        in_specs=[pl.BlockSpec(memory_space=pltpu.HBM)] * len(operands),
        out_specs=(whole, whole),
        scratch_shapes=[space(a.shape, a.dtype) for space, a in zip(spaces, operands)]
        + [pltpu.SemaphoreType.DMA((len(operands),))]
        + compute_scratch(
            tile_feats.shape[0], tile_feats.shape[1], narrow, wide, kernel_one.shape[0], inward_one.shape[1], inward_two.shape[1]),
        compiler_params=pltpu.CompilerParams(vmem_limit_bytes=60 * 1024 * 1024),
    )(*operands)
    if not direct:
        project, both = (
            lax.psum(lax.psum_scatter(g.reshape(rows, wide), "slide", scatter_dimension=0, tiled=True), "rep")
            for g in (halves[0], halves[1]))
        return features, both[:, :narrow].T, both[:, narrow:], project
    share = rows // slides
    inward, outward, project = pl.pallas_call(
        finish_kernel,
        out_shape=tuple(jax.ShapeDtypeStruct(d, jnp.float32) for d in ((narrow, share), (share, narrow), (share, wide))),
        in_specs=[whole],
        out_specs=(whole,) * 3,
        compiler_params=pltpu.CompilerParams(vmem_limit_bytes=60 * 1024 * 1024),
    )(exchange(halves, slides))
    return features, inward, outward, project


def solution(mesh):
    in_specs = (
        P(("slide", "rep"), None, None, None),
        P(("slide", "rep"), None, None, None),
        P(("slide", "rep"), None),
        P(("slide", "rep"), None),
        P(),
        P(),
        P(),
        P(),
        P(),
        P(),
        P(),
        P(),
        P(),
        P(),
    )
    out_specs = (
        P(("slide", "rep"), None, None, None),
        P(None, "slide"),
        P("slide", None),
        P("slide", None),
    )
    return jax.shard_map(
        per_device, mesh=mesh, in_specs=in_specs, out_specs=out_specs, check_vma=False
    )
```

```python
import functools

import jax
import jax.numpy as jnp
from jax import lax
from jax.experimental import pallas as pl
from jax.experimental.pallas import tpu as pltpu
from jax.sharding import PartitionSpec as P

MESH = pl.DeviceIdType.MESH


def routes(line):
    s = lax.axis_index("slide")
    r = lax.axis_index("rep")
    core, y = r % 2, r // 2
    x, z = s % 2, s // 2

    def quad_peer(d):
        return (z * 2 + (x + d // 2) % 2, ((y + d) % 2) * 2 + core)

    def line_peer(d):
        return (((z + d) % line) * 2 + x, r)

    def rep_peer(d):
        return (s, ((y + d // 2) % 2) * 2 + (core + d) % 2)

    return quad_peer, line_peer, rep_peer


def greet(line):
    quad_peer, line_peer, rep_peer = routes(line)
    barrier = pltpu.get_barrier_semaphore()
    peers = [rep_peer(d) for d in (1, 2, 3)] + [quad_peer(d) for d in (2, 3)] + [line_peer(d) for d in range(1, line)]
    for peer in peers:
        pl.semaphore_signal(barrier, inc=1, device_id=peer, device_id_type=MESH)


def exchange_part(line, halves, out, get_pair, put_sq, get_sq, put_ln, get_ln, mine_a, mine_b, put_a, get_a, put_b, get_b,
                    put_rep, get_rep, pair_sems, sq_sems, ln_sems, a_sems, b_sems, rep_sems):
    s = lax.axis_index("slide")
    r = lax.axis_index("rep")
    core, y = r % 2, r // 2
    x, z = s % 2, s // 2
    cut = put_sq.shape[-1]
    pair_peer = (s, y * 2 + 1 - core)

    quad_peer, line_peer, rep_peer = routes(line)

    def quad_spot(d):
        return ((x + d // 2) % 2) * 2 + (y + d) % 2

    pl.semaphore_wait(pltpu.get_barrier_semaphore(), line + 4)
    started = []

    def send(src, dst, sems, slot, peer):
        copy = pltpu.make_async_remote_copy(
            src_ref=src, dst_ref=dst, send_sem=sems.at[0, slot], recv_sem=sems.at[1, slot],
            device_id=peer, device_id_type=MESH)
        copy.start()
        started.append(copy)
        return copy

    def wide(value):
        return value.astype(jnp.float32)

    others = range(line - 1, 0, -1)
    pairs = {d: send(halves.at[1 - core, quad_spot(d)], get_pair.at[d], pair_sems, d, pair_peer) for d in (3, 2, 1, 0)}
    squares, lines = {}, {}
    for d in (3, 2, 1, 0):
        pairs[d].wait_recv()
        q = quad_spot(d)
        first = wide(halves[core, q, :, :, :cut]) + wide(get_pair[d, :, :, :cut])
        if d:
            put_sq[d - 1] = first.astype(jnp.bfloat16)
            squares[d] = send(put_sq.at[d - 1], get_sq.at[d - 1], sq_sems, d - 1, quad_peer(d))
        else:
            mine_a[...] = first
        for e in (*others, 0):
            at = (z + e) % line
            last = wide(halves[core, q, at, :, cut:]) + wide(get_pair[d, at, :, cut:])
            if e:
                put_ln[e - 1, q] = last.astype(jnp.bfloat16)
            else:
                mine_b[q] = last
    for e in others:
        lines[e] = send(put_ln.at[e - 1], get_ln.at[e - 1], ln_sems, e - 1, line_peer(e))
    for d in squares:
        squares[d].wait_recv()
    then = []
    for e in (*others, 0):
        at = (z + e) % line
        total_a = mine_a[at] + wide(get_sq[0, at]) + wide(get_sq[1, at]) + wide(get_sq[2, at])
        if e:
            put_a[e - 1] = total_a.astype(jnp.bfloat16)
            then.append(send(put_a.at[e - 1], get_a.at[e - 1], a_sems, e - 1, line_peer(e)))
    for e in lines:
        lines[e].wait_recv()
    for d in (3, 2, 1, 0):
        q = quad_spot(d)
        total_b = mine_b[q]
        for e in others:
            total_b = total_b + wide(get_ln[e - 1, q])
        if d:
            put_b[d - 1] = total_b.astype(jnp.bfloat16)
            then.append(send(put_b.at[d - 1], get_b.at[d - 1], b_sems, d - 1, quad_peer(d)))
    for copy in then:
        copy.wait_recv()
    for e in others:
        total_a = total_a + wide(get_a[e - 1])
    for d in (1, 2, 3):
        total_b = total_b + wide(get_b[d - 1])
    put_rep[:, :cut] = total_a.astype(jnp.bfloat16)
    put_rep[:, cut:] = total_b.astype(jnp.bfloat16)
    reps = {d: send(put_rep, get_rep.at[d - 1], rep_sems, d - 1, rep_peer(d)) for d in (3, 2, 1)}
    out[core, y] = put_rep[...]
    for d in (1, 3, 2):
        reps[d].wait_recv()
        out[(core + d) % 2, (y + d // 2) % 2] = get_rep[d - 1]
    for copy in started:
        copy.wait_send()


def exchange_scratch(line, part, width):
    cut = width // 3 * 2
    first, last, block = (part, cut), (part, width - cut), (part, width)
    bf16, f32 = jnp.bfloat16, jnp.float32
    buffers = [
        ((2, 4, line) + block, bf16), ((4, line) + block, bf16),
        ((3, line) + first, bf16), ((3, line) + first, bf16),
        ((line - 1, 4) + last, bf16), ((line - 1, 4) + last, bf16),
        ((line,) + first, f32), ((4,) + last, f32),
        ((line - 1,) + first, bf16), ((line - 1,) + first, bf16),
        ((3,) + last, bf16), ((3,) + last, bf16),
        (block, bf16), ((3,) + block, bf16),
    ]
    return [pltpu.VMEM(*b) for b in buffers] + [pltpu.SemaphoreType.DMA((2, n)) for n in (4, 3, line - 1, line - 1, 3, 3)]


def dot(a, b, contract=(1, 0)):
    return lax.dot_general(a, b, (((contract[0],), (contract[1],)), ((), ())), preferred_element_type=jnp.float32)


def centre_scale(values):
    offset = values - jnp.mean(values, axis=-1, keepdims=True)
    scale = lax.rsqrt(jnp.mean(offset * offset, axis=-1, keepdims=True) + 1e-06)
    return offset * scale, scale


def norm_back(grad, unit, scale):
    return scale * (grad - jnp.mean(grad, axis=-1, keepdims=True) - unit * jnp.mean(grad * unit, axis=-1, keepdims=True))


def gelu_rows(expand, hidden, slope, rows, columns):
    across = expand.shape[1] // columns

    def body(i, carry):
        here = pl.ds(pl.multiple_of(i * rows, rows), rows)
        for c in range(across):
            there = slice(c * columns, (c + 1) * columns)
            v = expand[here, there]
            below = 0.5 + 0.5 * lax.erf(v * 0.7071067811865476)
            hidden[here, there] = (v * below).astype(jnp.bfloat16)
            slope[here, there] = below + v * (jnp.exp(v * v * -0.5) * 0.3989422804014327)
        return carry

    lax.fori_loop(0, expand.shape[0] // rows, body, 0)


def side_sum(shifted, taps, out, flip):
    span, side = shifted.shape[0], shifted.shape[1]
    reach = span // 2
    for i in range(side):
        total = None
        for other in range(max(0, i - reach), min(side, i + reach + 1)):
            row = reach + (i - other if flip else other - i)
            for d in range(span):
                term = shifted[d, other] * taps[row, (span - 1 - d) if flip else d]
                total = term if total is None else total + term
        out[i] = total


def fetch(far, near, sems):
    fetches = [pltpu.make_async_copy(far[i], near[i], sems.at[i]) for i in range(len(far))]
    for i in (2, 3, 0, 4, 5, 6, 7, 8, 9, 10, 11, 12, 1, 13):
        fetches[i].start()
    return fetches


def compute_kernel(count, *refs):
    far, features, halves = refs[:count], refs[count], refs[count + 1]
    near, sems = refs[count + 2:2 * count + 2], refs[2 * count + 2]
    step(*near, features, halves, *refs[2 * count + 3:], fetch(far, near, sems))


def whole_kernel(count, line, *refs):
    far, features, got = refs[:count], refs[count], refs[count + 1]
    near, sems = refs[count + 2:2 * count + 2], refs[2 * count + 2]
    inner, (halves, *buffers) = refs[2 * count + 3:2 * count + 18], refs[2 * count + 18:]
    fetches = fetch(far, near, sems)
    greet(line)
    step(*near, features, halves, *inner, fetches)
    exchange_part(line, halves, got, *buffers)


def step(feats, cot, keep, plan, kernel_one, gain_one, inward_one, outward_one, gain_down, project, kernel_two,
         gain_two, inward_two, outward_two, features, halves, pad_one, shift_one, taps_one, conv_one, expand, hidden,
                   slope, pad_two, shift_two, taps_two, conv_two, rows_two, expand_two, hidden_two, slope_two, fetches):
    tiles, side, _, narrow = feats.shape
    half = side // 2
    wide = project.shape[1]
    span = kernel_one.shape[0]
    reach = span // 2
    rows, small = tiles * side * side, tiles * half * half
    f32, bf16 = jnp.float32, jnp.bfloat16
    def arrive(*which):
        for i in which:
            fetches[i].wait()

    arrive(2, 3)
    lives = []
    for t in range(tiles):
        place = sum(jnp.where(keep[0, p] == t, p, 0) for p in range(tiles))
        lives.append(jnp.where(place < plan[0, 0], 1.0, 0.0).astype(f32))

    arrive(0, 4)
    for d in range(span):
        taps_one[d] = jnp.broadcast_to(kernel_one[d].astype(f32)[:, None, :], (span, 8, narrow))
    pad_one[...] = jnp.zeros_like(pad_one)
    for t in range(tiles):
        pad_one[:, t, 8:8 + side, :] = feats[t].astype(f32) * lives[t]
    for d in range(span):
        shift_one[d] = pad_one[:, :, 8 + d - reach:8 + d - reach + side, :]
    side_sum(shift_one, taps_one, conv_one, False)
    arrive(5, 6, 7)
    unit, _ = centre_scale(conv_one[...].reshape(rows, narrow))
    normed = (unit * gain_one[...].astype(f32)[None]).astype(bf16)
    plain = pad_one[:, :, 8:8 + side, :].reshape(rows, narrow).astype(bf16)
    to = lax.broadcasted_iota(jnp.int32, (rows, rows), 0)
    column_pair, rest = to & (half - 1), to >> (half.bit_length() - 1)
    tile, rest = rest & (tiles - 1), rest >> (tiles.bit_length() - 1)
    row_pair, rest = rest & (half - 1), rest >> (half.bit_length() - 1)
    source = ((row_pair * 2 + (rest >> 1)) * tiles + tile) * side + column_pair * 2 + (rest & 1)
    order = jnp.where(lax.broadcasted_iota(jnp.int32, (rows, rows), 1) == source, 1.0, 0.0).astype(bf16)
    normed = dot(order, normed).astype(bf16)
    plain = dot(order, plain)
    expand[...] = dot(normed, inward_one[...])
    gelu_rows(expand, hidden, slope, 16, expand.shape[1])
    arrive(8, 9, 10, 11, 12, 1, 13)
    section = (plain + dot(hidden[...], outward_one[...], (1, 1))).astype(bf16).astype(f32)
    unit_down, scale_down = centre_scale(section)
    gain = gain_down[...].astype(f32)[None]
    down = (unit_down * gain).astype(bf16)
    merged = sum(dot(down[q * small:(q + 1) * small], project[q * narrow:(q + 1) * narrow]) for q in range(4)).astype(bf16).astype(f32)

    for d in range(span):
        taps_two[d] = jnp.broadcast_to(kernel_two[d].astype(f32)[:, None, :], (span, 8, wide))
    lane = lax.broadcasted_iota(jnp.int32, (half, tiles * half, wide), 1) & (half - 1)

    def second_conv(values, flip):
        pad_two[...] = jnp.zeros_like(pad_two)
        pad_two[:, 8:8 + tiles * half, :] = values.reshape(half, tiles * half, wide)
        for d in range(span):
            at = lane + (d - reach)
            moved = pad_two[:, 8 + d - reach:8 + d - reach + tiles * half, :]
            shift_two[d] = jnp.where((at >= 0) & (at < half), moved, 0.0).reshape(half, tiles * half // 8, 8, wide)
        side_sum(shift_two, taps_two, conv_two, flip)
        return conv_two[...].reshape(small, wide)

    unit_two, scale_two = centre_scale(second_conv(merged, False))
    second_gain = gain_two[...].astype(f32)[None]
    normed_two = (unit_two * second_gain).astype(bf16)
    expand_two[...] = dot(normed_two, inward_two[...])
    gelu_rows(expand_two, hidden_two, slope_two, 16, expand_two.shape[1] // 2)
    rows_two[...] = merged + dot(hidden_two[...], outward_two[...])
    for t in range(tiles):
        for i in range(half):
            at = (i * tiles + t) * half
            features[t, i] = (rows_two[at:at + half] * lives[t]).astype(bf16)
    for t in range(tiles):
        for i in range(half):
            at = (i * tiles + t) * half
            rows_two[at:at + half] = cot[t, i].astype(f32) * lives[t]
    cotangent = rows_two[...]
    back = dot(cotangent.astype(bf16), outward_two[...], (1, 1)).astype(bf16).astype(f32)
    back = (slope_two[...] * back).astype(bf16)
    back = dot(back, inward_two[...], (1, 1)).astype(bf16).astype(f32)
    back = second_conv(norm_back(back * second_gain, unit_two, scale_two), True)
    back_merged = (cotangent + back).astype(bf16)

    spots, line, part = halves.shape[1:4]

    def put(where, start, value):
        for at in range(0, value.shape[0], part):
            whole = (start + at) // part
            halves[where, whole % spots, whole // spots] = value[at:at + part].astype(halves.dtype)

    grad_project = jnp.concatenate([dot(down[q * small:(q + 1) * small], back_merged, (0, 0)) for q in range(4)], axis=0)
    put(0, 0, grad_project)
    back_down = jnp.concatenate([dot(back_merged, project[q * narrow:(q + 1) * narrow], (1, 1)) for q in range(4)], axis=0)
    back_down = back_down.astype(bf16).astype(f32)
    back_section = norm_back(back_down * gain, unit_down, scale_down).astype(bf16)
    grad_outward = dot(hidden[...], back_section, (0, 0))
    back_hidden = dot(back_section, outward_one[...]).astype(bf16).astype(f32)
    back_expand = (slope[...] * back_hidden).astype(bf16)
    grad_inward = dot(back_expand, normed, (0, 0))
    put(1, 0, jnp.concatenate([grad_inward, grad_outward], axis=1))


def compute_scratch(tiles, side, narrow, wide, span, inner, inner_two):
    half = side // 2
    rows, small = tiles * side * side, tiles * half * half
    f32, bf16 = jnp.float32, jnp.bfloat16
    return [
        pltpu.VMEM((side, tiles, side + 16, narrow), f32),
        pltpu.VMEM((span, side, tiles, side, narrow), f32),
        pltpu.VMEM((span, span, 8, narrow), f32),
        pltpu.VMEM((side, tiles, side, narrow), f32),
        pltpu.VMEM((rows, inner), f32),
        pltpu.VMEM((rows, inner), bf16),
        pltpu.VMEM((rows, inner), f32),
        pltpu.VMEM((half, tiles * half + 16, wide), f32),
        pltpu.VMEM((span, half, tiles * half // 8, 8, wide), f32),
        pltpu.VMEM((span, span, 8, wide), f32),
        pltpu.VMEM((half, tiles * half // 8, 8, wide), f32),
        pltpu.VMEM((small, wide), f32),
        pltpu.VMEM((small, inner_two), f32),
        pltpu.VMEM((small, inner_two), bf16),
        pltpu.VMEM((small, inner_two), f32),
    ]


def finish_kernel(early, got, features, inward, outward, project):
    features[...] = early[...]
    part, narrow = got.shape[2], outward.shape[1]
    both = jnp.concatenate([got[1, y].astype(jnp.float32) for y in range(2)], axis=0)
    inward[...] = both[:, :narrow].T
    outward[...] = both[:, narrow:]
    for y in range(2):
        project[y * part:(y + 1) * part] = got[0, y].astype(jnp.float32)


def fits(slides, reps, rows, wide):
    return wide % 384 == 0 and reps == 4 and slides % 2 == 0 and slides > 2 and rows % (slides * 32) == 0


def per_device(tile_feats, cotangent, keep_list, tile_plan, kernel_one, gain_one, inward_one, outward_one, gain_down,
               project_down, kernel_two, gain_two, inward_two, outward_two):
    slides, reps = lax.axis_size("slide"), lax.axis_size("rep")
    rows, wide = project_down.shape
    narrow = tile_feats.shape[3]
    direct = fits(slides, reps, rows, wide)
    operands = (tile_feats, cotangent, keep_list, tile_plan, kernel_one, gain_one, inward_one, outward_one.T, gain_down,
                project_down, kernel_two, gain_two, inward_two, outward_two)
    spaces = [pltpu.SMEM if a.dtype == jnp.int32 else pltpu.VMEM for a in operands]
    whole = pl.BlockSpec(memory_space=pltpu.VMEM)
    scratch = (
        [space(a.shape, a.dtype) for space, a in zip(spaces, operands)]
        + [pltpu.SemaphoreType.DMA((len(operands),))]
        + compute_scratch(
            tile_feats.shape[0], tile_feats.shape[1], narrow, wide, kernel_one.shape[0], inward_one.shape[1], inward_two.shape[1]))
    far = [pl.BlockSpec(memory_space=pl.ANY)] * len(operands)
    kept = jax.ShapeDtypeStruct(cotangent.shape, jnp.bfloat16)
    if not direct:
        features, halves = pl.pallas_call(
            functools.partial(compute_kernel, len(operands)),
            out_shape=(kept, jax.ShapeDtypeStruct((2, 1, 1, rows, wide), jnp.float32)),
            in_specs=far,
            out_specs=(whole, whole),
            scratch_shapes=scratch,
            compiler_params=pltpu.CompilerParams(vmem_limit_bytes=60 * 1024 * 1024),
        )(*operands)
        project, both = (
            lax.psum(lax.psum_scatter(g.reshape(rows, wide), "slide", scatter_dimension=0, tiled=True), "rep")
            for g in (halves[0], halves[1]))
        return features, both[:, :narrow].T, both[:, narrow:], project
    line, share = slides // 2, rows // slides
    features, got = pl.pallas_call(
        functools.partial(whole_kernel, len(operands), line),
        out_shape=(kept, jax.ShapeDtypeStruct((2, 2, share // 2, wide), jnp.bfloat16)),
        in_specs=far,
        out_specs=(whole, whole),
        scratch_shapes=scratch + exchange_scratch(line, share // 2, wide),
        compiler_params=pltpu.CompilerParams(collective_id=0, has_side_effects=True, vmem_limit_bytes=60 * 1024 * 1024),
    )(*operands)
    return pl.pallas_call(
        finish_kernel,
        out_shape=(kept,) + tuple(jax.ShapeDtypeStruct(d, jnp.float32) for d in ((narrow, share), (share, narrow), (share, wide))),
        in_specs=[whole] * 2,
        out_specs=(whole,) * 4,
        compiler_params=pltpu.CompilerParams(vmem_limit_bytes=60 * 1024 * 1024),
    )(features, got)


def solution(mesh):
    in_specs = (
        P(("slide", "rep"), None, None, None),
        P(("slide", "rep"), None, None, None),
        P(("slide", "rep"), None),
        P(("slide", "rep"), None),
        P(),
        P(),
        P(),
        P(),
        P(),
        P(),
        P(),
        P(),
        P(),
        P(),
    )
    out_specs = (
        P(("slide", "rep"), None, None, None),
        P(None, "slide"),
        P("slide", None),
        P("slide", None),
    )
    return jax.shard_map(
        per_device, mesh=mesh, in_specs=in_specs, out_specs=out_specs, check_vma=False
    )
```

```python
import functools

import jax
import jax.numpy as jnp
from jax import lax
from jax.experimental import pallas as pl
from jax.experimental.pallas import tpu as pltpu
from jax.sharding import PartitionSpec as P

MESH = pl.DeviceIdType.MESH


def routes(line):
    s = lax.axis_index("slide")
    r = lax.axis_index("rep")
    core, y = r % 2, r // 2
    x, z = s % 2, s // 2

    def quad_peer(d):
        return (z * 2 + (x + d // 2) % 2, ((y + d) % 2) * 2 + core)

    def line_peer(d):
        return (((z + d) % line) * 2 + x, r)

    def rep_peer(d):
        return (s, ((y + d // 2) % 2) * 2 + (core + d) % 2)

    return quad_peer, line_peer, rep_peer


def greet(line):
    quad_peer, line_peer, rep_peer = routes(line)
    barrier = pltpu.get_barrier_semaphore()
    peers = [rep_peer(d) for d in (1, 2, 3)] + [quad_peer(d) for d in (2, 3)] + [line_peer(d) for d in range(1, line)]
    for peer in peers:
        pl.semaphore_signal(barrier, inc=1, device_id=peer, device_id_type=MESH)


def exchange_part(line, halves, out, get_pair, put_sq, get_sq, put_ln, get_ln, mine_a, mine_b, put_a, get_a, put_b, get_b,
                    put_rep, get_rep, pair_sems, sq_sems, ln_sems, a_sems, b_sems, rep_sems):
    s = lax.axis_index("slide")
    r = lax.axis_index("rep")
    core, y = r % 2, r // 2
    x, z = s % 2, s // 2
    cut = put_sq.shape[-1]
    pair_peer = (s, y * 2 + 1 - core)

    quad_peer, line_peer, rep_peer = routes(line)

    def quad_spot(d):
        return ((x + d // 2) % 2) * 2 + (y + d) % 2

    pl.semaphore_wait(pltpu.get_barrier_semaphore(), line + 4)
    started = []

    def send(src, dst, sems, slot, peer):
        copy = pltpu.make_async_remote_copy(
            src_ref=src, dst_ref=dst, send_sem=sems.at[0, slot], recv_sem=sems.at[1, slot],
            device_id=peer, device_id_type=MESH)
        copy.start()
        started.append(copy)
        return copy

    def wide(value):
        return value.astype(jnp.float32)

    others = range(line - 1, 0, -1)
    pairs = {d: send(halves.at[1 - core, quad_spot(d)], get_pair.at[d], pair_sems, d, pair_peer) for d in (3, 2, 1, 0)}
    squares, lines = {}, {}
    for d in (3, 2, 1, 0):
        pairs[d].wait_recv()
        q = quad_spot(d)
        first = wide(halves[core, q, :, :, :cut]) + wide(get_pair[d, :, :, :cut])
        if d:
            put_sq[d - 1] = first.astype(jnp.bfloat16)
            squares[d] = send(put_sq.at[d - 1], get_sq.at[d - 1], sq_sems, d - 1, quad_peer(d))
        else:
            mine_a[...] = first
        for e in (*others, 0):
            at = (z + e) % line
            last = wide(halves[core, q, at, :, cut:]) + wide(get_pair[d, at, :, cut:])
            if e:
                put_ln[e - 1, q] = last.astype(jnp.bfloat16)
                lines[e, d] = send(put_ln.at[e - 1, q], get_ln.at[e - 1, q], ln_sems, (e - 1) * 4 + d, line_peer(e))
            else:
                mine_b[q] = last
    for d in squares:
        squares[d].wait_recv()
    then = []
    for e in (*others, 0):
        at = (z + e) % line
        total_a = mine_a[at] + wide(get_sq[0, at]) + wide(get_sq[1, at]) + wide(get_sq[2, at])
        if e:
            put_a[e - 1] = total_a.astype(jnp.bfloat16)
            then.append(send(put_a.at[e - 1], get_a.at[e - 1], a_sems, e - 1, line_peer(e)))
    for e in lines:
        lines[e].wait_recv()
    for d in (3, 2, 1, 0):
        q = quad_spot(d)
        total_b = mine_b[q]
        for e in others:
            total_b = total_b + wide(get_ln[e - 1, q])
        if d:
            put_b[d - 1] = total_b.astype(jnp.bfloat16)
            then.append(send(put_b.at[d - 1], get_b.at[d - 1], b_sems, d - 1, quad_peer(d)))
    for copy in then:
        copy.wait_recv()
    for e in others:
        total_a = total_a + wide(get_a[e - 1])
    for d in (1, 2, 3):
        total_b = total_b + wide(get_b[d - 1])
    put_rep[:, :cut] = total_a.astype(jnp.bfloat16)
    put_rep[:, cut:] = total_b.astype(jnp.bfloat16)
    reps = {d: send(put_rep, get_rep.at[d - 1], rep_sems, d - 1, rep_peer(d)) for d in (3, 2, 1)}
    out[core, y] = put_rep[...]
    for d in (1, 3, 2):
        reps[d].wait_recv()
        out[(core + d) % 2, (y + d // 2) % 2] = get_rep[d - 1]
    for copy in started:
        copy.wait_send()


def exchange_scratch(line, part, width):
    cut = width // 3 * 2
    first, last, block = (part, cut), (part, width - cut), (part, width)
    bf16, f32 = jnp.bfloat16, jnp.float32
    buffers = [
        ((2, 4, line) + block, bf16), ((4, line) + block, bf16),
        ((3, line) + first, bf16), ((3, line) + first, bf16),
        ((line - 1, 4) + last, bf16), ((line - 1, 4) + last, bf16),
        ((line,) + first, f32), ((4,) + last, f32),
        ((line - 1,) + first, bf16), ((line - 1,) + first, bf16),
        ((3,) + last, bf16), ((3,) + last, bf16),
        (block, bf16), ((3,) + block, bf16),
    ]
    return [pltpu.VMEM(*b) for b in buffers] + [pltpu.SemaphoreType.DMA((2, n)) for n in (4, 3, 4 * (line - 1), line - 1, 3, 3)]


def dot(a, b, contract=(1, 0)):
    return lax.dot_general(a, b, (((contract[0],), (contract[1],)), ((), ())), preferred_element_type=jnp.float32)


def centre_scale(values):
    offset = values - jnp.mean(values, axis=-1, keepdims=True)
    scale = lax.rsqrt(jnp.mean(offset * offset, axis=-1, keepdims=True) + 1e-06)
    return offset * scale, scale


def norm_back(grad, unit, scale):
    return scale * (grad - jnp.mean(grad, axis=-1, keepdims=True) - unit * jnp.mean(grad * unit, axis=-1, keepdims=True))


def gelu_rows(expand, hidden, slope, rows, columns):
    across = expand.shape[1] // columns

    def body(i, carry):
        here = pl.ds(pl.multiple_of(i * rows, rows), rows)
        for c in range(across):
            there = slice(c * columns, (c + 1) * columns)
            v = expand[here, there]
            below = 0.5 + 0.5 * lax.erf(v * 0.7071067811865476)
            hidden[here, there] = (v * below).astype(jnp.bfloat16)
            slope[here, there] = below + v * (jnp.exp(v * v * -0.5) * 0.3989422804014327)
        return carry

    lax.fori_loop(0, expand.shape[0] // rows, body, 0)


def side_sum(shifted, taps, out, flip):
    span, side = shifted.shape[0], shifted.shape[1]
    reach = span // 2
    for i in range(side):
        total = None
        for other in range(max(0, i - reach), min(side, i + reach + 1)):
            row = reach + (i - other if flip else other - i)
            for d in range(span):
                term = shifted[d, other] * taps[row, (span - 1 - d) if flip else d]
                total = term if total is None else total + term
        out[i] = total


def fetch(far, near, sems):
    fetches = [pltpu.make_async_copy(far[i], near[i], sems.at[i]) for i in range(len(far))]
    for i in (2, 3, 0, 4, 5, 6, 7, 8, 9, 10, 11, 12, 1, 13):
        fetches[i].start()
    return fetches


def compute_kernel(count, *refs):
    far, features, halves = refs[:count], refs[count], refs[count + 1]
    near, sems = refs[count + 2:2 * count + 2], refs[2 * count + 2]
    step(*near, features, halves, *refs[2 * count + 3:], fetch(far, near, sems))


def whole_kernel(count, line, *refs):
    far, features, got = refs[:count], refs[count], refs[count + 1]
    near, sems = refs[count + 2:2 * count + 2], refs[2 * count + 2]
    inner, (halves, *buffers) = refs[2 * count + 3:2 * count + 18], refs[2 * count + 18:]
    fetches = fetch(far, near, sems)
    greet(line)
    step(*near, features, halves, *inner, fetches)
    exchange_part(line, halves, got, *buffers)


def step(feats, cot, keep, plan, kernel_one, gain_one, inward_one, outward_one, gain_down, project, kernel_two,
         gain_two, inward_two, outward_two, features, halves, pad_one, shift_one, taps_one, conv_one, expand, hidden,
                   slope, pad_two, shift_two, taps_two, conv_two, rows_two, expand_two, hidden_two, slope_two, fetches):
    tiles, side, _, narrow = feats.shape
    half = side // 2
    wide = project.shape[1]
    span = kernel_one.shape[0]
    reach = span // 2
    rows, small = tiles * side * side, tiles * half * half
    f32, bf16 = jnp.float32, jnp.bfloat16
    def arrive(*which):
        for i in which:
            fetches[i].wait()

    arrive(2, 3)
    lives = []
    for t in range(tiles):
        place = sum(jnp.where(keep[0, p] == t, p, 0) for p in range(tiles))
        lives.append(jnp.where(place < plan[0, 0], 1.0, 0.0).astype(f32))

    arrive(0, 4)
    for d in range(span):
        taps_one[d] = jnp.broadcast_to(kernel_one[d].astype(f32)[:, None, :], (span, 8, narrow))
    pad_one[...] = jnp.zeros_like(pad_one)
    for t in range(tiles):
        pad_one[:, t, 8:8 + side, :] = feats[t].astype(f32) * lives[t]
    for d in range(span):
        shift_one[d] = pad_one[:, :, 8 + d - reach:8 + d - reach + side, :]
    side_sum(shift_one, taps_one, conv_one, False)
    arrive(5, 6, 7)
    unit, _ = centre_scale(conv_one[...].reshape(rows, narrow))
    normed = (unit * gain_one[...].astype(f32)[None]).astype(bf16)
    plain = pad_one[:, :, 8:8 + side, :].reshape(rows, narrow).astype(bf16)
    to = lax.broadcasted_iota(jnp.int32, (rows, rows), 0)
    column_pair, rest = to & (half - 1), to >> (half.bit_length() - 1)
    tile, rest = rest & (tiles - 1), rest >> (tiles.bit_length() - 1)
    row_pair, rest = rest & (half - 1), rest >> (half.bit_length() - 1)
    source = ((row_pair * 2 + (rest >> 1)) * tiles + tile) * side + column_pair * 2 + (rest & 1)
    order = jnp.where(lax.broadcasted_iota(jnp.int32, (rows, rows), 1) == source, 1.0, 0.0).astype(bf16)
    normed = dot(order, normed).astype(bf16)
    plain = dot(order, plain)
    expand[...] = dot(normed, inward_one[...])
    gelu_rows(expand, hidden, slope, 16, expand.shape[1])
    arrive(8, 9, 10, 11, 12, 1, 13)
    section = (plain + dot(hidden[...], outward_one[...], (1, 1))).astype(bf16).astype(f32)
    unit_down, scale_down = centre_scale(section)
    gain = gain_down[...].astype(f32)[None]
    down = (unit_down * gain).astype(bf16)
    merged = sum(dot(down[q * small:(q + 1) * small], project[q * narrow:(q + 1) * narrow]) for q in range(4)).astype(bf16).astype(f32)

    for d in range(span):
        taps_two[d] = jnp.broadcast_to(kernel_two[d].astype(f32)[:, None, :], (span, 8, wide))
    lane = lax.broadcasted_iota(jnp.int32, (half, tiles * half, wide), 1) & (half - 1)

    def second_conv(values, flip):
        pad_two[...] = jnp.zeros_like(pad_two)
        pad_two[:, 8:8 + tiles * half, :] = values.reshape(half, tiles * half, wide)
        for d in range(span):
            at = lane + (d - reach)
            moved = pad_two[:, 8 + d - reach:8 + d - reach + tiles * half, :]
            shift_two[d] = jnp.where((at >= 0) & (at < half), moved, 0.0).reshape(half, tiles * half // 8, 8, wide)
        side_sum(shift_two, taps_two, conv_two, flip)
        return conv_two[...].reshape(small, wide)

    unit_two, scale_two = centre_scale(second_conv(merged, False))
    second_gain = gain_two[...].astype(f32)[None]
    normed_two = (unit_two * second_gain).astype(bf16)
    expand_two[...] = dot(normed_two, inward_two[...])
    gelu_rows(expand_two, hidden_two, slope_two, 16, expand_two.shape[1] // 2)
    rows_two[...] = merged + dot(hidden_two[...], outward_two[...])
    for t in range(tiles):
        for i in range(half):
            at = (i * tiles + t) * half
            features[t, i] = (rows_two[at:at + half] * lives[t]).astype(bf16)
    for t in range(tiles):
        for i in range(half):
            at = (i * tiles + t) * half
            rows_two[at:at + half] = cot[t, i].astype(f32) * lives[t]
    cotangent = rows_two[...]
    back = dot(cotangent.astype(bf16), outward_two[...], (1, 1)).astype(bf16).astype(f32)
    back = (slope_two[...] * back).astype(bf16)
    back = dot(back, inward_two[...], (1, 1)).astype(bf16).astype(f32)
    back = second_conv(norm_back(back * second_gain, unit_two, scale_two), True)
    back_merged = (cotangent + back).astype(bf16)

    spots, line, part = halves.shape[1:4]

    def put(where, start, value):
        for at in range(0, value.shape[0], part):
            whole = (start + at) // part
            halves[where, whole % spots, whole // spots] = value[at:at + part].astype(halves.dtype)

    grad_project = jnp.concatenate([dot(down[q * small:(q + 1) * small], back_merged, (0, 0)) for q in range(4)], axis=0)
    put(0, 0, grad_project)
    back_down = jnp.concatenate([dot(back_merged, project[q * narrow:(q + 1) * narrow], (1, 1)) for q in range(4)], axis=0)
    back_down = back_down.astype(bf16).astype(f32)
    back_section = norm_back(back_down * gain, unit_down, scale_down).astype(bf16)
    grad_outward = dot(hidden[...], back_section, (0, 0))
    back_hidden = dot(back_section, outward_one[...]).astype(bf16).astype(f32)
    back_expand = (slope[...] * back_hidden).astype(bf16)
    grad_inward = dot(back_expand, normed, (0, 0))
    put(1, 0, jnp.concatenate([grad_inward, grad_outward], axis=1))


def compute_scratch(tiles, side, narrow, wide, span, inner, inner_two):
    half = side // 2
    rows, small = tiles * side * side, tiles * half * half
    f32, bf16 = jnp.float32, jnp.bfloat16
    return [
        pltpu.VMEM((side, tiles, side + 16, narrow), f32),
        pltpu.VMEM((span, side, tiles, side, narrow), f32),
        pltpu.VMEM((span, span, 8, narrow), f32),
        pltpu.VMEM((side, tiles, side, narrow), f32),
        pltpu.VMEM((rows, inner), f32),
        pltpu.VMEM((rows, inner), bf16),
        pltpu.VMEM((rows, inner), f32),
        pltpu.VMEM((half, tiles * half + 16, wide), f32),
        pltpu.VMEM((span, half, tiles * half // 8, 8, wide), f32),
        pltpu.VMEM((span, span, 8, wide), f32),
        pltpu.VMEM((half, tiles * half // 8, 8, wide), f32),
        pltpu.VMEM((small, wide), f32),
        pltpu.VMEM((small, inner_two), f32),
        pltpu.VMEM((small, inner_two), bf16),
        pltpu.VMEM((small, inner_two), f32),
    ]


def finish_kernel(early, got, features, inward, outward, project):
    features[...] = early[...]
    part, narrow = got.shape[2], outward.shape[1]
    both = jnp.concatenate([got[1, y].astype(jnp.float32) for y in range(2)], axis=0)
    inward[...] = both[:, :narrow].T
    outward[...] = both[:, narrow:]
    for y in range(2):
        project[y * part:(y + 1) * part] = got[0, y].astype(jnp.float32)


def fits(slides, reps, rows, wide):
    return wide % 384 == 0 and reps == 4 and slides % 2 == 0 and slides > 2 and rows % (slides * 32) == 0


def per_device(tile_feats, cotangent, keep_list, tile_plan, kernel_one, gain_one, inward_one, outward_one, gain_down,
               project_down, kernel_two, gain_two, inward_two, outward_two):
    slides, reps = lax.axis_size("slide"), lax.axis_size("rep")
    rows, wide = project_down.shape
    narrow = tile_feats.shape[3]
    direct = fits(slides, reps, rows, wide)
    operands = (tile_feats, cotangent, keep_list, tile_plan, kernel_one, gain_one, inward_one, outward_one.T, gain_down,
                project_down, kernel_two, gain_two, inward_two, outward_two)
    spaces = [pltpu.SMEM if a.dtype == jnp.int32 else pltpu.VMEM for a in operands]
    whole = pl.BlockSpec(memory_space=pltpu.VMEM)
    scratch = (
        [space(a.shape, a.dtype) for space, a in zip(spaces, operands)]
        + [pltpu.SemaphoreType.DMA((len(operands),))]
        + compute_scratch(
            tile_feats.shape[0], tile_feats.shape[1], narrow, wide, kernel_one.shape[0], inward_one.shape[1], inward_two.shape[1]))
    far = [pl.BlockSpec(memory_space=pl.ANY)] * len(operands)
    kept = jax.ShapeDtypeStruct(cotangent.shape, jnp.bfloat16)
    if not direct:
        features, halves = pl.pallas_call(
            functools.partial(compute_kernel, len(operands)),
            out_shape=(kept, jax.ShapeDtypeStruct((2, 1, 1, rows, wide), jnp.float32)),
            in_specs=far,
            out_specs=(whole, whole),
            scratch_shapes=scratch,
            compiler_params=pltpu.CompilerParams(vmem_limit_bytes=60 * 1024 * 1024),
        )(*operands)
        project, both = (
            lax.psum(lax.psum_scatter(g.reshape(rows, wide), "slide", scatter_dimension=0, tiled=True), "rep")
            for g in (halves[0], halves[1]))
        return features, both[:, :narrow].T, both[:, narrow:], project
    line, share = slides // 2, rows // slides
    features, got = pl.pallas_call(
        functools.partial(whole_kernel, len(operands), line),
        out_shape=(kept, jax.ShapeDtypeStruct((2, 2, share // 2, wide), jnp.bfloat16)),
        in_specs=far,
        out_specs=(whole, whole),
        scratch_shapes=scratch + exchange_scratch(line, share // 2, wide),
        compiler_params=pltpu.CompilerParams(collective_id=0, has_side_effects=True, vmem_limit_bytes=60 * 1024 * 1024),
    )(*operands)
    return pl.pallas_call(
        finish_kernel,
        out_shape=(kept,) + tuple(jax.ShapeDtypeStruct(d, jnp.float32) for d in ((narrow, share), (share, narrow), (share, wide))),
        in_specs=[whole] * 2,
        out_specs=(whole,) * 4,
        compiler_params=pltpu.CompilerParams(vmem_limit_bytes=60 * 1024 * 1024),
    )(features, got)


def solution(mesh):
    in_specs = (
        P(("slide", "rep"), None, None, None),
        P(("slide", "rep"), None, None, None),
        P(("slide", "rep"), None),
        P(("slide", "rep"), None),
        P(),
        P(),
        P(),
        P(),
        P(),
        P(),
        P(),
        P(),
        P(),
        P(),
    )
    out_specs = (
        P(("slide", "rep"), None, None, None),
        P(None, "slide"),
        P("slide", None),
        P("slide", None),
    )
    return jax.shard_map(
        per_device, mesh=mesh, in_specs=in_specs, out_specs=out_specs, check_vma=False
    )
```
